256 devices in a mesh: gx: 16 (over z, core), gy: 16 (over y, x).
Axes of the slice: x: 4, y: 4, z: 8, core: 2. Of those that a mesh axis runs over, the one named last changes fastest.
Arguments:
- populations: float32 [19, 256, 128, 256], P(None, 'gx', 'gy'), may hold values from 0 to 0.5, as said below
- relax_rate: float32 [256, 128, 256], P('gx', 'gy'), may hold values from 0.6 to 1.6
- solid_mask: int32 [256, 128, 256], P('gx', 'gy'), may hold values 0 or 1
- singular_values: float32 [64], replicated, may hold values from 1 to 4
- basis: float32 [64, 3, 128, 64, 128], P(None, None, 'gx', 'gy'), may hold values from -60 to 60
- snapshots: float32 [15, 3, 128, 64, 128], P(None, None, 'gx', 'gy'), may hold values from -60 to 60
Outputs:
- populations_out: float32 [19, 256, 128, 256], P(None, 'gx', 'gy')
- upper_factor: float32 [80, 80], replicated
- new_basis: float32 [80, 3, 128, 64, 128], P(None, None, 'gx', 'gy')
The draws below stay inside these ranges and needn't reach their ends.
Inputs may be any that keep to these rules, and one draw needn't show every extreme that they name: `populations`: each entry is w_i times a factor between 0.7 and 1.3.
All inputs are finite; a program needn't handle non-finite values. No bound on the sum of `solid_mask` on one device may be relied on, other than what follows from the above.
Results may differ from the reference program's by a relative error of at most 0.00012.
Values sent between devices are 32-bit elements; how exact they have to be, the bound alone decides.
A program may use at most 128 MiB of HBM per device.

```python
import math
import jax
import jax.numpy as jnp
from jax import lax

NVEL = 19
SUBSTEPS = 2
RANK = 64
SNAPS = 16
COLS = 80
NX = 256
NY = 128
NZ = 256
NXC = 128
NYC = 64
NZC = 128
ROWS_ALL = 3145728


weight_table = [1.0 / 3.0] + [1.0 / 18.0] * 6 + [1.0 / 36.0] * 12


def draw_populations(key, part):
    shape = (NVEL, NX, NY, NZ)
    weights = jnp.array(weight_table, jnp.float32)[:, None, None, None]
    factor = 1.0 + 0.3 * jax.random.uniform(key, shape, jnp.float32, -1.0, 1.0)
    return weights * factor


def scaled_rows(key, count):
    shape = (count, 3, NXC, NYC, NZC)
    ix = jnp.arange(NXC, dtype=jnp.float32)[:, None, None] / (NXC - 1)
    iy = jnp.arange(NYC, dtype=jnp.float32)[None, :, None] / (NYC - 1)
    spread = 10.0 ** ((ix + iy) * 0.5)
    first = jax.random.fold_in(key, 11)
    values = jnp.clip(jax.random.normal(first, shape, jnp.float32), -6.0, 6.0)
    return values * spread


def draw_basis(key, part):
    return scaled_rows(jax.random.fold_in(key, 101), RANK)


def draw_snapshots(key, part):
    return scaled_rows(jax.random.fold_in(key, 202), SNAPS - 1)


def touch_ends(values, rng, low, largest):
    extent = values.shape
    spot = [jax.random.randint(jax.random.fold_in(rng, axis), (), 0, extent[axis]) for axis in range(len(extent))]
    values = values.at[tuple(spot)].set(low)
    longest = extent.index(max(extent))
    spot[longest] = (spot[longest] + 1) % extent[longest]
    return values.at[tuple(spot)].set(largest)


def block_levels(own_key, shape, shards, low, high):
    level = 1.0
    for dim, shards_of in shards:
        steps = jax.random.uniform(jax.random.fold_in(jax.random.fold_in(own_key, 6), dim), (shards_of,), jnp.float32, low / len(shards), high / len(shards))
        level = level * jnp.repeat(jnp.exp(steps), shape[dim] // shards_of).reshape((-1,) + (1,) * (len(shape) - 1 - dim))
    return level


def setup_inputs(seed: int = 0) -> dict:
    splits = jax.random.split(jax.random.key(seed), 7)
    return {
        "populations": draw_populations(jax.random.fold_in(splits[6], 71), 0),
        "relax_rate": jnp.clip(0.6 + 1.0 * jax.random.uniform(splits[1], (NX, NY, NZ), jnp.float32) ** block_levels(splits[1], (NX, NY, NZ), ((0, 16), (1, 16)), -0.2, 0.2), 0.6, 1.6),
        "solid_mask": touch_ends((jax.random.randint(splits[2], (NX, NY, NZ), 0, 8) < 1).astype(jnp.int32), jax.random.fold_in(splits[2], 1), 0, 1),
        "singular_values": jnp.clip(jnp.exp(jax.random.uniform(splits[3], (RANK,), jnp.float32, math.log(1.0), math.log(4.0))), 1.0, 4.0),
        "basis": draw_basis(jax.random.fold_in(splits[6], 71), 0),
        "snapshots": draw_snapshots(jax.random.fold_in(splits[6], 71), 0),
    }


velocity_table = [(0, 0, 0), (1, 0, 0), (-1, 0, 0), (0, 1, 0), (0, -1, 0), (0, 0, 1), (0, 0, -1), (1, 1, 0), (-1, -1, 0), (1, -1, 0), (-1, 1, 0), (1, 0, 1), (-1, 0, -1), (1, 0, -1), (-1, 0, 1), (0, 1, 1), (0, -1, -1), (0, 1, -1), (0, -1, 1)]
weight_table = [1.0 / 3.0] + [1.0 / 18.0] * 6 + [1.0 / 36.0] * 12
reverse_table = [0, 2, 1, 4, 3, 6, 5, 8, 7, 10, 9, 12, 11, 14, 13, 16, 15, 18, 17]
speed_scale = 10.0

def moments(field):
    highest = lax.Precision.HIGHEST
    density = jnp.sum(field, axis=0)
    comps = []
    for axis_id in range(3):
        column = jnp.array([v[axis_id] for v in velocity_table], jnp.float32)
        comps.append(jnp.tensordot(column, field, axes=1, precision=highest) / density)
    return (density, comps)

def collide(field, relax_rate, solid_mask):
    density, comps = moments(field)
    usq = comps[0] * comps[0] + comps[1] * comps[1] + comps[2] * comps[2]
    result = []
    for index in range(19):
        vel = velocity_table[index]
        along = vel[0] * comps[0] + vel[1] * comps[1] + vel[2] * comps[2]
        equil = weight_table[index] * density * (1.0 + 3.0 * along + 4.5 * along * along - 1.5 * usq)
        relaxed = field[index] + relax_rate * (equil - field[index])
        result.append(jnp.where(solid_mask > 0, field[reverse_table[index]], relaxed))
    return result

def reference(populations, relax_rate, solid_mask, singular_values, basis, snapshots):
    field = populations
    for step in range(SUBSTEPS):
        post = collide(field, relax_rate, solid_mask)
        field = jnp.stack([jnp.roll(post[i], velocity_table[i], axis=(0, 1, 2)) for i in range(19)])
    density, comps = moments(field)
    fluid = (solid_mask == 0).astype(jnp.float32)
    vel = jnp.stack([c * fluid for c in comps])
    coarse = speed_scale * jnp.mean(vel.reshape(3, NXC, 2, NYC, 2, NZC, 2), axis=(2, 4, 6))
    stacked = jnp.concatenate([singular_values[:, None, None, None, None] * basis, snapshots, coarse[None]], axis=0)
    flat = stacked.reshape(COLS, ROWS_ALL)
    scaled = flat * (1.0 / ROWS_ALL ** 0.5)
    gram = lax.dot_general(scaled.astype(jnp.float32), scaled.astype(jnp.float32), (((1,), (1,)), ((), ())), precision=lax.Precision.HIGHEST, preferred_element_type=jnp.float32)
    lower = jnp.linalg.cholesky(gram)
    rotated = lax.linalg.triangular_solve(lower, flat, left_side=True, lower=True)
    return (field, lower.T, rotated.reshape(COLS, 3, NXC, NYC, NZC))
```

```python
import functools

import jax
import jax.numpy as jnp
from jax import lax
from jax.experimental import pallas as pl
from jax.experimental.pallas import tpu as pltpu
from jax.sharding import PartitionSpec as P

MESH = pl.DeviceIdType.MESH
HIGHEST = lax.Precision.HIGHEST
F32 = jnp.float32
BF16 = jnp.bfloat16

VELOCITY = [
    (0, 0, 0),
    (1, 0, 0),
    (-1, 0, 0),
    (0, 1, 0),
    (0, -1, 0),
    (0, 0, 1),
    (0, 0, -1),
    (1, 1, 0),
    (-1, -1, 0),
    (1, -1, 0),
    (-1, 1, 0),
    (1, 0, 1),
    (-1, 0, -1),
    (1, 0, -1),
    (-1, 0, 1),
    (0, 1, 1),
    (0, -1, -1),
    (0, 1, -1),
    (0, -1, 1),
]
SPEED_SCALE = 10.0

ORDER = [1, 7, 9, 11, 13, 2, 8, 10, 12, 14, 0, 3, 4, 5, 6, 15, 16, 17, 18]
PLACE = [ORDER.index(i) for i in range(19)]
Y_UP = [3, 7, 10, 15, 17]
Y_DOWN = [4, 8, 9, 16, 18]
CORNERS = [(7, 16, 1, 1), (8, 1, -1, -1), (9, 16, 1, -1), (10, 1, -1, 1)]

NX, NY, NZ = 16, 8, 256
XC, YC, ZC = 8, 4, 128
COLS, RANK, OLD = 80, 64, 15
ROWS = 3 * XC * YC
HALO0 = 8


def flow(field):
    plus = [field[i] + field[i + 1] for i in range(1, 19, 2)]
    diff = [field[i] - field[i + 1] for i in range(1, 19, 2)]
    rho = field[0]
    for s in plus:
        rho = rho + s
    comps = []
    for axis in range(3):
        total = None
        for p, d in enumerate(diff):
            c = VELOCITY[2 * p + 1][axis]
            if c:
                total = d if total is None else (total + d if c > 0 else total - d)
        comps.append(total)
    inv = 1.0 / rho
    return rho, [c * inv for c in comps]


def collide(field, rate, solid):
    rho, vel = flow(field)
    tri = [3.0 * u for u in vel]
    base = 1.0 - 1.5 * (vel[0] * vel[0] + vel[1] * vel[1] + vel[2] * vel[2])
    post = [None] * 19
    face = rho * (1.0 / 18.0)
    edge = rho * (1.0 / 36.0)
    rest = rho * (1.0 / 3.0) * base
    post[0] = jnp.where(solid, field[0], field[0] + rate * (rest - field[0]))
    for i in range(1, 19, 2):
        along = None
        for axis in range(3):
            c = VELOCITY[i][axis]
            if c:
                along = (
                    tri[axis]
                    if along is None
                    else (along + tri[axis] if c > 0 else along - tri[axis])
                )
        weight = face if i < 7 else edge
        even = weight * (base + 0.5 * (along * along))
        odd = weight * along
        fp, fm = field[i], field[i + 1]
        post[i] = jnp.where(solid, fm, fp + rate * ((even + odd) - fp))
        post[i + 1] = jnp.where(solid, fp, fm + rate * ((even - odd) - fm))
    return post


def arrive(post_ref, up_ref, down_ref, x):
    row = lax.broadcasted_iota(jnp.int32, (NY, NZ), 0)
    field = []
    for i, (cx, cy, cz) in enumerate(VELOCITY):
        v = post_ref[PLACE[i], x + 1 - cx]
        if cy == 1:
            halo = up_ref[Y_UP.index(i), pl.ds(x + HALO0 - cx, 1), :]
            v = jnp.where(row == 0, halo, pltpu.roll(v, 1, axis=0))
        elif cy == -1:
            halo = down_ref[Y_DOWN.index(i), pl.ds(x + HALO0 - cx, 1), :]
            v = jnp.where(row == NY - 1, halo, pltpu.roll(v, NY - 1, axis=0))
        if cz == 1:
            v = pltpu.roll(v, 1, axis=1)
        elif cz == -1:
            v = pltpu.roll(v, NZ - 1, axis=1)
        field.append(v)
    return field


def split(x):
    hi = x.astype(BF16)
    lo = (x - hi.astype(F32)).astype(BF16)
    return hi, lo


def dot(a, b, ca, cb, precision=None):
    return lax.dot_general(
        a, b, (((ca,), (cb,)), ((), ())), precision=precision, preferred_element_type=F32
    )


def scale_row(ref, sv_ref):
    ref[...] = jnp.ones_like(ref)
    ref[0:1, 0:RANK] = sv_ref[...]
    return ref[0:1, :]


def main_kernel(
    nx,
    ny,
    pops_hbm,
    rate_hbm,
    mask_hbm,
    sv_ref,
    basis_hbm,
    snaps_hbm,
    field_hbm,
    coarse_ref,
    inverse_ref,
    upper_ref,
    border_ref,
    pops,
    rate,
    mask,
    stack,
    post_a,
    post_b,
    out_up,
    out_down,
    in_up,
    in_down,
    in_corner,
    vel,
    pooled,
    gram,
    parts,
    recv_a,
    send_b,
    recv_b,
    recv_c,
    vec_a,
    vec_b,
    vec_in_a,
    vec_in_b,
    scale,
    plane_sem,
    load_sem,
    store_sem,
    halo_send,
    halo_recv,
    red_send,
    red_recv,
):
    mx, my = lax.axis_index("gx"), lax.axis_index("gy")
    owners = COLS // 8
    posts = (post_a, post_b)

    def shifted(dx, dy):
        return (lax.rem(mx + (dx + nx), nx), lax.rem(my + (dy + ny), ny))

    def load_plane(x):
        return pltpu.make_async_copy(pops_hbm.at[:, x], pops.at[:, x], plane_sem.at[x])

    loads = [
        pltpu.make_async_copy(rate_hbm, rate, load_sem.at[0]),
        pltpu.make_async_copy(mask_hbm, mask, load_sem.at[1]),
        pltpu.make_async_copy(basis_hbm, stack.at[pl.ds(0, RANK)], load_sem.at[2]),
        pltpu.make_async_copy(snaps_hbm, stack.at[pl.ds(RANK, OLD)], load_sem.at[3]),
    ]
    loads[0].start()
    loads[1].start()

    @pl.loop(0, NX)
    def _(x):
        load_plane(x).start()

    loads[2].start()
    loads[3].start()

    barrier = pltpu.get_barrier_semaphore()

    @pl.loop(1, nx)
    def _(j):
        pl.semaphore_signal(
            barrier, inc=1, device_id=(lax.rem(mx + j, nx), my), device_id_type=MESH
        )

    @pl.loop(1, ny)
    def _(j):
        pl.semaphore_signal(
            barrier, inc=1, device_id=(mx, lax.rem(my + j, ny)), device_id_type=MESH
        )

    for dx in (-1, 1):
        for dy in (-1, 1):
            pl.semaphore_signal(barrier, inc=1, device_id=shifted(dx, dy), device_id_type=MESH)

    stack[COLS - 1] = jnp.zeros((ROWS, ZC), F32)

    def put(post, step, x):
        for i in range(19):
            posts[step][PLACE[i], x + 1] = post[i]
        for p, i in enumerate(Y_UP):
            out_up[step, p, pl.ds(x, 1), :] = post[i][NY - 1 : NY, :]
        for p, i in enumerate(Y_DOWN):
            out_down[step, p, pl.ds(x, 1), :] = post[i][0:1, :]

    def halo(step):
        post = posts[step]
        inner = pl.ds(HALO0, NX)
        moves = [
            (post.at[pl.ds(0, 5), NX], post.at[pl.ds(0, 5), 0], (1, 0)),
            (post.at[pl.ds(5, 5), 1], post.at[pl.ds(5, 5), NX + 1], (-1, 0)),
            (out_up.at[step], in_up.at[step, :, inner, :], (0, 1)),
            (out_down.at[step], in_down.at[step, :, inner, :], (0, -1)),
        ]
        for c, (i, plane, dx, dy) in enumerate(CORNERS):
            moves.append((post.at[PLACE[i], plane], in_corner.at[step, c], (dx, dy)))
        return [
            pltpu.make_async_remote_copy(
                src_ref=src,
                dst_ref=dst,
                send_sem=halo_send.at[step, k],
                recv_sem=halo_recv.at[step, k],
                device_id=shifted(*to),
                device_id_type=MESH,
            )
            for k, (src, dst, to) in enumerate(moves)
        ]

    def land(step):
        for c, (i, plane, dx, dy) in enumerate(CORNERS):
            at = HALO0 - 1 if dx == 1 else HALO0 + NX
            if dy == 1:
                in_up[step, Y_UP.index(i), at : at + 1, :] = in_corner[step, c, NY - 1 : NY, :]
            else:
                in_down[step, Y_DOWN.index(i), at : at + 1, :] = in_corner[step, c, 0:1, :]

    loads[0].wait()
    loads[1].wait()

    @pl.loop(0, NX)
    def _(x):
        load_plane(x).wait()
        field = [pops[i, x] for i in range(19)]
        put(collide(field, rate[x], mask[x] > 0), 0, x)

    pl.semaphore_wait(barrier, (nx - 1) + (ny - 1) + 4)
    first = halo(0)
    for copy in first:
        copy.start()

    loads[2].wait()
    loads[3].wait()
    rows = stack.reshape(COLS * ROWS, ZC)
    gram[...] = jnp.zeros_like(gram)
    wide = 8

    @pl.loop(0, ROWS // wide)
    def _(c):
        tall = jnp.concatenate(
            [rows[pl.ds(c * wide + w, COLS, stride=ROWS), :] for w in range(wide)], axis=1
        )
        hi, lo = split(tall)
        gram[:, 0:COLS] += dot(jnp.concatenate([hi, lo], axis=0), hi, 1, 1)

    parts[0:COLS, :] = gram[0:COLS, :]
    low = jnp.concatenate([gram[COLS : 2 * COLS, :], jnp.zeros((ZC - COLS, ZC), F32)], axis=0)
    parts[...] = gram[0:COLS, :] + low[0:COLS] + jnp.transpose(low)[0:COLS]

    def to_owner(j):
        peer = lax.rem(mx + j, nx)
        chunk = lax.rem(peer, owners)
        return peer, pltpu.make_async_remote_copy(
            src_ref=parts.at[pl.ds(pl.multiple_of(chunk * 8, 8), 8)],
            dst_ref=recv_a.at[mx],
            send_sem=red_send.at[0],
            recv_sem=red_recv.at[0],
            device_id=(peer, my),
            device_id_type=MESH,
        )

    @pl.loop(1, nx)
    def _(j):
        peer, copy = to_owner(j)

        @pl.when(peer < owners)
        def _():
            copy.start()

    own = pl.ds(pl.multiple_of(lax.rem(mx, owners) * 8, 8), 8)
    recv_a[mx] = parts[own, :]

    for copy in first:
        copy.wait_recv()
    land(0)

    @pl.loop(0, NX)
    def _(x):
        field = arrive(post_a, in_up.at[0], in_down.at[0], x)
        put(collide(field, rate[x], mask[x] > 0), 1, x)

    second = halo(1)
    for copy in second:
        copy.start()

    def all_along(src, dst, k, axis):
        def copy(j):
            if axis == 0:
                peer = (lax.rem(mx + j, nx), my)
            else:
                peer = (mx, lax.rem(my + j, ny))
            return pltpu.make_async_remote_copy(
                src_ref=src,
                dst_ref=dst,
                send_sem=red_send.at[k],
                recv_sem=red_recv.at[k],
                device_id=peer,
                device_id_type=MESH,
            )

        return copy

    def start_all(copy, count):
        @pl.loop(1, count)
        def _(j):
            copy(j).start()

    def wait_for(ref, sem):
        pltpu.make_async_copy(ref, ref, sem).wait()

    def total(ref, count):
        value = ref[0]
        for j in range(1, count):
            value = value + ref[j]
        return value

    ring_b = all_along(send_b.at[0], recv_b.at[my], 1, 1)
    ring_c = all_along(send_b.at[1], recv_c.at[mx], 2, 0)

    @pl.when(mx < owners)
    def _():
        wait_for(recv_a.at[pl.ds(0, nx - 1)], red_recv.at[0])
        value = total(recv_a, nx)
        send_b[0] = value
        recv_b[my] = value
        start_all(ring_b, ny)

    for copy in second:
        copy.wait_recv()
    land(1)

    def store_plane(x):
        return pltpu.make_async_copy(pops.at[:, x], field_hbm.at[:, x], store_sem.at[x])

    @pl.loop(0, XC)
    def _(xc):
        sums = [None] * 3
        for half in range(2):
            x = 2 * xc + half
            field = arrive(post_b, in_up.at[1], in_down.at[1], x)
            for i in range(19):
                pops[i, x] = field[i]
            store_plane(x).start()
            fluid = mask[x] == 0
            for a, u in enumerate(flow(field)[1]):
                u = jnp.where(fluid, u, 0.0)
                sums[a] = u if half == 0 else sums[a] + u
        for a in range(3):
            vel[pl.ds(pl.multiple_of(a * XC * NY + xc * NY, NY), NY), :] = sums[a]

    @pl.when(mx < owners)
    def _():
        wait_for(recv_b.at[pl.ds(0, ny - 1)], red_recv.at[1])
        value = total(recv_b, ny)
        send_b[1] = value
        recv_c[mx] = value
        start_all(ring_c, nx)

    fine = lax.broadcasted_iota(jnp.int32, (NZ, ZC), 0)
    pair = lax.broadcasted_iota(jnp.int32, (NZ, ZC), 1)
    pick = jnp.where(fine // 2 == pair, SPEED_SCALE / 8.0, 0.0).astype(F32)
    pooled[...] = dot(vel[...], pick, 1, 0, HIGHEST)
    coarse = pooled[pl.ds(0, ROWS, stride=2), :] + pooled[pl.ds(1, ROWS, stride=2), :]
    coarse_ref[...] = coarse
    stack[COLS - 1] = coarse

    vec_a[...] = jnp.zeros_like(vec_a)

    @pl.loop(0, ROWS // wide)
    def _(c):
        value = vec_a[0:COLS, :]
        for w in range(wide):
            r = c * wide + w
            value = value + rows[pl.ds(r, COLS, stride=ROWS), :] * coarse_ref[pl.ds(r, 1), :]
        vec_a[0:COLS, :] = value

    last = dot(jnp.ones((8, ZC), F32), vec_a[...], 1, 1, HIGHEST)
    vec_b[0] = last
    vec_in_a[mx] = last
    ring_d = all_along(vec_b.at[0], vec_in_a.at[mx], 3, 0)
    start_all(ring_d, nx)

    @pl.when(mx < owners)
    def _():
        wait_for(recv_c.at[pl.ds(0, owners - 1)], red_recv.at[2])

    @pl.when(mx >= owners)
    def _():
        wait_for(recv_c.at[pl.ds(0, owners)], red_recv.at[2])

    row = lax.broadcasted_iota(jnp.int32, (COLS, ZC), 0)
    lane = lax.broadcasted_iota(jnp.int32, (COLS, ZC), 1)
    srow = scale_row(scale, sv_ref)
    scol = jnp.sum(jnp.where(row == lane, srow, 0.0), axis=1, keepdims=True)
    per_row = 1.0 / (all_rows(nx, ny))
    whole = jnp.concatenate([recv_c[c] for c in range(owners)], axis=0)
    whole = whole * (srow * scol) * per_row
    whole = jnp.where((row == COLS - 1) & (lane == COLS - 1), 1.0, whole)

    row8 = lax.broadcasted_iota(jnp.int32, (8, ZC), 0)
    lane8 = lax.broadcasted_iota(jnp.int32, (8, ZC), 1)

    def eight(b, state):
        a, e = state
        r, t = a[0:8], e[0:8]
        for j in range(8):
            pivot = r[j : j + 1, j : j + 1]
            inv = lax.rsqrt(pivot)
            inv = inv * (1.5 - 0.5 * pivot * inv * inv)
            factor = jnp.where(row8[:, 0:1] > j, r[:, j : j + 1] * inv, 0.0)
            urow, trow = r[j : j + 1] * inv, t[j : j + 1] * inv
            r = jnp.where(row8 == j, urow, r - factor * urow)
            t = jnp.where(row8 == j, trow, t - factor * trow)
        r = jnp.where((lane8 >= row8) & (lane8 < COLS - 8 * b), r, 0.0)
        at = pl.ds(pl.multiple_of(8 * b, 8), 8)
        upper_ref[at, :] = pltpu.roll(r, 8 * b, axis=1)
        inverse_ref[at, :] = t
        change = dot(r, jnp.concatenate([r, t], axis=1), 0, 0, HIGHEST)
        zero = jnp.zeros((8, ZC), F32)
        a = jnp.concatenate([a[8:] - change[8:COLS, 0:ZC], zero], axis=0)
        e = jnp.concatenate([e[8:] - change[8:COLS, ZC:], zero], axis=0)
        return pltpu.roll(a, ZC - 8, axis=1), e

    state = (whole, (row == lane).astype(F32))
    half = (owners + 1) // 2
    state = lax.fori_loop(0, half, eight, state)

    wait_for(vec_in_a.at[pl.ds(0, nx - 1)], red_recv.at[3])
    value = total(vec_in_a, nx)
    vec_b[1] = value
    vec_in_b[my] = value
    ring_e = all_along(vec_b.at[1], vec_in_b.at[my], 4, 1)
    start_all(ring_e, ny)

    lax.fori_loop(half, owners, eight, state)

    wait_for(vec_in_b.at[pl.ds(0, ny - 1)], red_recv.at[4])
    border_ref[...] = total(vec_in_b, ny) * srow * per_row

    @pl.loop(0, NX)
    def _(x):
        store_plane(x).wait()

    for copy in first + second:
        copy.wait_send()

    @pl.when(mx < owners)
    def _():
        wait_for(recv_a.at[pl.ds(0, owners - 1)], red_send.at[0])
        wait_for(recv_b.at[pl.ds(0, ny - 1)], red_send.at[1])
        wait_for(recv_a.at[pl.ds(0, nx - 1)], red_send.at[2])

    @pl.when(mx >= owners)
    def _():
        wait_for(recv_a.at[pl.ds(0, owners)], red_send.at[0])

    wait_for(vec_in_a.at[pl.ds(0, nx - 1)], red_send.at[3])
    wait_for(vec_in_b.at[pl.ds(0, ny - 1)], red_send.at[4])


def all_rows(nx, ny):
    return float(ROWS * ZC * nx * ny)


def finish_kernel(
    field_hbm,
    sv_ref,
    basis_hbm,
    snaps_hbm,
    coarse_ref,
    inverse_ref,
    upper_ref,
    border_ref,
    pops_hbm,
    factor_ref,
    new_hbm,
    stack,
    fresh,
    left,
    scale,
    load_sem,
    store_sem,
):
    wide = 8
    copies = [
        pltpu.make_async_copy(basis_hbm, stack.at[pl.ds(0, RANK)], load_sem.at[0]),
        pltpu.make_async_copy(snaps_hbm, stack.at[pl.ds(RANK, OLD)], load_sem.at[1]),
        pltpu.make_async_copy(field_hbm, pops_hbm, load_sem.at[2]),
    ]
    for copy in copies:
        copy.start()
    stack[COLS - 1] = coarse_ref[...]

    row = lax.broadcasted_iota(jnp.int32, (COLS, ZC), 0)
    lane = lax.broadcasted_iota(jnp.int32, (COLS, ZC), 1)
    inverse = inverse_ref[...]
    border = border_ref[...]
    lane8 = lax.broadcasted_iota(jnp.int32, (8, ZC), 1)
    old = jnp.where(lane8 < COLS - 1, border, 0.0)
    tall = jnp.concatenate([inverse, jnp.zeros((ZC - COLS, ZC), F32)], axis=0)
    lrow = dot(old, tall, 1, 1, HIGHEST)
    lrow = jnp.where(lane8 < COLS - 1, lrow, 0.0)
    wide_old = jnp.concatenate([old] * (ZC // 8), axis=0)
    lcol = dot(inverse, wide_old, 1, 1, HIGHEST)
    left_over = border[0:1, COLS - 1 : COLS] - jnp.sum(lrow[0:1] * lrow[0:1], axis=1, keepdims=True)
    inv = lax.rsqrt(left_over)
    inv = inv * (1.5 - 0.5 * left_over * inv * inv)
    diag = left_over * inv
    end = dot(lrow, tall, 1, 0, HIGHEST)[0:1]
    end = jnp.where(lane[0:1] == COLS - 1, inv, -end * inv)
    inverse = jnp.where(row == COLS - 1, end, inverse)
    final = jnp.where(lane == COLS - 1, jnp.where(row == COLS - 1, diag, lcol), upper_ref[...])
    final = jnp.where((row == COLS - 1) & (lane < COLS - 1), 0.0, final)
    factor_ref[...] = final[:, 0:COLS]

    inverse = inverse * scale_row(scale, sv_ref)
    hi = inverse.astype(BF16).astype(F32)
    lo = inverse - hi
    none = jnp.zeros_like(hi)
    hi, lo = jnp.concatenate([hi, none], axis=1), jnp.concatenate([lo, none], axis=1)
    placed = hi + pltpu.roll(lo, COLS, axis=1) + pltpu.roll(hi, 2 * COLS, axis=1)
    left[...] = placed.astype(BF16)

    rows = stack.reshape(COLS * ROWS, ZC)
    made = fresh.reshape(COLS * ROWS, ZC)

    def store(c):
        part = pl.ds(pl.multiple_of(c * wide, wide), wide)
        return pltpu.make_async_copy(fresh.at[:, part], new_hbm.at[:, part], store_sem.at[c])

    copies[0].wait()
    copies[1].wait()

    @pl.loop(0, ROWS // wide)
    def _(c):
        tall = jnp.concatenate(
            [rows[pl.ds(c * wide + w, COLS, stride=ROWS), :] for w in range(wide)], axis=1
        )
        hi, lo = split(tall)
        result = dot(left[:, 0 : 3 * COLS], jnp.concatenate([hi, hi, lo], axis=0), 1, 0)
        for w in range(wide):
            made[pl.ds(c * wide + w, COLS, stride=ROWS), :] = result[:, w * ZC : (w + 1) * ZC]
        store(c).start()

    @pl.loop(0, ROWS // wide)
    def _(c):
        store(c).wait()

    copies[2].wait()


def on_device(nx, ny, pops, rate, mask, sv, basis, snaps):
    sv = sv.reshape(1, RANK)
    basis = basis.reshape(RANK, ROWS, ZC)
    snaps = snaps.reshape(OLD, ROWS, ZC)
    anywhere = pl.BlockSpec(memory_space=pl.ANY)
    here = pl.BlockSpec(memory_space=pltpu.VMEM)
    owners = COLS // 8

    def f32(*shape):
        return jax.ShapeDtypeStruct(shape, F32)

    def vmem(*shape):
        return pltpu.VMEM(shape, F32)

    dma = pltpu.SemaphoreType.DMA
    field, coarse, inverse, upper, border = pl.pallas_call(
        functools.partial(main_kernel, nx, ny),
        out_shape=(
            f32(19, NX, NY, NZ),
            f32(ROWS, ZC),
            f32(COLS, ZC),
            f32(COLS, ZC),
            f32(8, ZC),
        ),
        in_specs=[anywhere, anywhere, anywhere, here, anywhere, anywhere],
        out_specs=(anywhere, here, here, here, here),
        scratch_shapes=[
            vmem(19, NX, NY, NZ),
            vmem(NX, NY, NZ),
            pltpu.VMEM((NX, NY, NZ), jnp.int32),
            vmem(COLS, ROWS, ZC),
            vmem(19, NX + 2, NY, NZ),
            vmem(19, NX + 2, NY, NZ),
            vmem(2, 5, NX, NZ),
            vmem(2, 5, NX, NZ),
            vmem(2, 5, NX + 16, NZ),
            vmem(2, 5, NX + 16, NZ),
            vmem(2, 4, NY, NZ),
            vmem(3 * XC * NY, NZ),
            vmem(3 * XC * NY, ZC),
            vmem(2 * COLS, ZC),
            vmem(COLS, ZC),
            vmem(nx, 8, ZC),
            vmem(2, 8, ZC),
            vmem(ny, 8, ZC),
            vmem(owners, 8, ZC),
            vmem(ZC, ZC),
            vmem(2, 8, ZC),
            vmem(nx, 8, ZC),
            vmem(ny, 8, ZC),
            vmem(8, ZC),
            dma((NX,)),
            dma((4,)),
            dma((NX,)),
            dma((2, 8)),
            dma((2, 8)),
            dma((5,)),
            dma((5,)),
        ],
        compiler_params=pltpu.CompilerParams(
            collective_id=0, has_side_effects=True, vmem_limit_bytes=40 * 2**20
        ),
        name="substeps",
    )(pops, rate, mask, sv, basis, snaps)
    out, factor, fresh = pl.pallas_call(
        finish_kernel,
        out_shape=(f32(19, NX, NY, NZ), f32(COLS, COLS), f32(COLS, ROWS, ZC)),
        in_specs=[anywhere, here, anywhere, anywhere, here, here, here, here],
        out_specs=(anywhere, here, anywhere),
        scratch_shapes=[
            vmem(COLS, ROWS, ZC),
            vmem(COLS, ROWS, ZC),
            pltpu.VMEM((COLS, 2 * ZC), BF16),
            vmem(8, ZC),
            dma((3,)),
            dma((ROWS // 8,)),
        ],
        compiler_params=pltpu.CompilerParams(vmem_limit_bytes=40 * 2**20),
        name="finish",
    )(field, sv, basis, snaps, coarse, inverse, upper, border)
    return out, factor, fresh.reshape(COLS, 3, XC, YC, ZC)


def solution(mesh):
    return jax.shard_map(
        functools.partial(on_device, mesh.shape["gx"], mesh.shape["gy"]),
        mesh=mesh,
        in_specs=(
            P(None, "gx", "gy", None),
            P("gx", "gy", None),
            P("gx", "gy", None),
            P(),
            P(None, None, "gx", "gy", None),
            P(None, None, "gx", "gy", None),
        ),
        out_specs=(P(None, "gx", "gy", None), P(), P(None, None, "gx", "gy", None)),
        check_vma=False,
    )
```

```python
import functools

import jax
import jax.numpy as jnp
from jax import lax
from jax.experimental import pallas as pl
from jax.experimental.pallas import tpu as pltpu
from jax.sharding import PartitionSpec as P

MESH = pl.DeviceIdType.MESH
HIGHEST = lax.Precision.HIGHEST
F32 = jnp.float32
BF16 = jnp.bfloat16

VELOCITY = [
    (0, 0, 0),
    (1, 0, 0),
    (-1, 0, 0),
    (0, 1, 0),
    (0, -1, 0),
    (0, 0, 1),
    (0, 0, -1),
    (1, 1, 0),
    (-1, -1, 0),
    (1, -1, 0),
    (-1, 1, 0),
    (1, 0, 1),
    (-1, 0, -1),
    (1, 0, -1),
    (-1, 0, 1),
    (0, 1, 1),
    (0, -1, -1),
    (0, 1, -1),
    (0, -1, 1),
]
SPEED_SCALE = 10.0

ORDER = [1, 7, 9, 11, 13, 2, 8, 10, 12, 14, 0, 3, 4, 5, 6, 15, 16, 17, 18]
PLACE = [ORDER.index(i) for i in range(19)]
Y_UP = [3, 7, 10, 15, 17]
Y_DOWN = [4, 8, 9, 16, 18]
CORNERS = [(7, 16, 1, 1), (8, 1, -1, -1), (9, 16, 1, -1), (10, 1, -1, 1)]

NX, NY, NZ = 16, 8, 256
XC, YC, ZC = 8, 4, 128
COLS, RANK, OLD = 80, 64, 15
ROWS = 3 * XC * YC
PITCH = ROWS + 8
HALO0 = 8


def flow(field):
    plus = [field[i] + field[i + 1] for i in range(1, 19, 2)]
    diff = [field[i] - field[i + 1] for i in range(1, 19, 2)]
    rho = field[0]
    for s in plus:
        rho = rho + s
    comps = []
    for axis in range(3):
        total = None
        for p, d in enumerate(diff):
            c = VELOCITY[2 * p + 1][axis]
            if c:
                total = d if total is None else (total + d if c > 0 else total - d)
        comps.append(total)
    inv = 1.0 / rho
    return rho, [c * inv for c in comps]


def collide(field, rate, solid):
    rho, vel = flow(field)
    tri = [3.0 * u for u in vel]
    base = 1.0 - 1.5 * (vel[0] * vel[0] + vel[1] * vel[1] + vel[2] * vel[2])
    post = [None] * 19
    face = rho * (1.0 / 18.0)
    edge = rho * (1.0 / 36.0)
    rest = rho * (1.0 / 3.0) * base
    post[0] = jnp.where(solid, field[0], field[0] + rate * (rest - field[0]))
    for i in range(1, 19, 2):
        along = None
        for axis in range(3):
            c = VELOCITY[i][axis]
            if c:
                along = (
                    tri[axis]
                    if along is None
                    else (along + tri[axis] if c > 0 else along - tri[axis])
                )
        weight = face if i < 7 else edge
        even = weight * (base + 0.5 * (along * along))
        odd = weight * along
        fp, fm = field[i], field[i + 1]
        post[i] = jnp.where(solid, fm, fp + rate * ((even + odd) - fp))
        post[i + 1] = jnp.where(solid, fp, fm + rate * ((even - odd) - fm))
    return post


def arrive(post_ref, up_ref, down_ref, x):
    row = lax.broadcasted_iota(jnp.int32, (NY, NZ), 0)
    field = []
    for i, (cx, cy, cz) in enumerate(VELOCITY):
        v = post_ref[PLACE[i], x + 1 - cx]
        if cy == 1:
            halo = up_ref[Y_UP.index(i), pl.ds(x + HALO0 - cx, 1), :]
            v = jnp.where(row == 0, halo, pltpu.roll(v, 1, axis=0))
        elif cy == -1:
            halo = down_ref[Y_DOWN.index(i), pl.ds(x + HALO0 - cx, 1), :]
            v = jnp.where(row == NY - 1, halo, pltpu.roll(v, NY - 1, axis=0))
        if cz == 1:
            v = pltpu.roll(v, 1, axis=1)
        elif cz == -1:
            v = pltpu.roll(v, NZ - 1, axis=1)
        field.append(v)
    return field


def split(x):
    hi = x.astype(BF16)
    lo = (x - hi.astype(F32)).astype(BF16)
    return hi, lo


def dot(a, b, ca, cb, precision=None):
    return lax.dot_general(
        a, b, (((ca,), (cb,)), ((), ())), precision=precision, preferred_element_type=F32
    )


def split3(x):
    hi = x.astype(BF16).astype(F32)
    mid = (x - hi).astype(BF16).astype(F32)
    return hi, mid, x - hi - mid


def outer8(r, t):
    h, m, l = split3(jnp.concatenate([r, t], axis=1))
    rh, rm, rl = h[:, 0:ZC], m[:, 0:ZC], l[:, 0:ZC]
    a = jnp.concatenate([rh, rh, rh, rm, rm, rl], axis=0).astype(BF16)
    b = jnp.concatenate([h, m, l, h, m, h], axis=0).astype(BF16)
    return dot(a, b, 0, 0)


def eliminate(rows, extra, first):
    d = [
        [jnp.broadcast_to(rows[i][:, first + j : first + j + 1], (1, ZC)) for j in range(i + 1)]
        for i in range(8)
    ]
    r, t = list(rows), list(extra)
    for j in range(8):
        inv = lax.rsqrt(d[j][j])
        r[j] = r[j] * inv
        t[j] = t[j] * inv
        col = [None if i <= j else d[i][j] * inv for i in range(8)]
        for i in range(j + 1, 8):
            for k in range(j + 1, i + 1):
                d[i][k] = d[i][k] - col[i] * col[k]
            r[i] = r[i] - col[i] * r[j]
            t[i] = t[i] - col[i] * t[j]
    return jnp.concatenate(r, axis=0), jnp.concatenate(t, axis=0)


def factor_block(b, work, inverse, upper):
    row8 = lax.broadcasted_iota(jnp.int32, (8, ZC), 0)
    lane8 = lax.broadcasted_iota(jnp.int32, (8, ZC), 1)
    o = 8 * b
    r, t = eliminate(
        [work[o + i : o + i + 1, :] for i in range(8)],
        [inverse[o + i : o + i + 1, :] for i in range(8)],
        o,
    )
    r = jnp.where(lane8 >= row8 + o, r, 0.0)
    upper[o : o + 8, :] = r
    inverse[o : o + 8, :] = t
    if o + 8 < COLS:
        change = outer8(r, t)
        work[o + 8 : COLS, :] = work[o + 8 : COLS, :] - change[o + 8 : COLS, 0:ZC]
        inverse[o + 8 : COLS, :] = inverse[o + 8 : COLS, :] - change[o + 8 : COLS, ZC:]


def main_kernel(
    nx,
    ny,
    pops_hbm,
    rate_hbm,
    mask_hbm,
    sv_hbm,
    basis_hbm,
    snaps_hbm,
    field_out,
    fresh,
    coarse_ref,
    inverse_ref,
    upper_ref,
    border_ref,
    pops,
    rate,
    mask,
    stack,
    post_a,
    post_b,
    out_up,
    out_down,
    in_up,
    in_down,
    in_corner,
    vel,
    pooled,
    gram,
    parts,
    recv_a,
    send_b,
    recv_b,
    recv_c,
    sums8,
    vec_b,
    vec_in_a,
    vec_in_b,
    sv,
    scale,
    work,
    left,
    plane_sem,
    load_sem,
    halo_send,
    halo_recv,
    red_send,
    red_recv,
):
    mx, my = lax.axis_index("gx"), lax.axis_index("gy")
    owners = COLS // 8
    posts = (post_a, post_b)

    def shifted(dx, dy):
        return (lax.rem(mx + (dx + nx), nx), lax.rem(my + (dy + ny), ny))

    def load_plane(x):
        return pltpu.make_async_copy(pops_hbm.at[:, x], pops.at[:, x], plane_sem.at[x])

    loads = [
        pltpu.make_async_copy(rate_hbm, rate, load_sem.at[0]),
        pltpu.make_async_copy(mask_hbm, mask, load_sem.at[1]),
        pltpu.make_async_copy(basis_hbm, stack.at[pl.ds(0, RANK), pl.ds(0, ROWS)], load_sem.at[2]),
        pltpu.make_async_copy(snaps_hbm, stack.at[pl.ds(RANK, OLD), pl.ds(0, ROWS)], load_sem.at[3]),
        pltpu.make_async_copy(sv_hbm, sv, load_sem.at[4]),
    ]

    @pl.loop(0, NX)
    def _(x):
        load_plane(x).start()

    loads[0].start()
    loads[1].start()

    loads[2].start()
    loads[3].start()
    loads[4].start()

    barrier = pltpu.get_barrier_semaphore()

    @pl.loop(1, nx)
    def _(j):
        pl.semaphore_signal(
            barrier, inc=1, device_id=(lax.rem(mx + j, nx), my), device_id_type=MESH
        )

    @pl.loop(1, ny)
    def _(j):
        pl.semaphore_signal(
            barrier, inc=1, device_id=(mx, lax.rem(my + j, ny)), device_id_type=MESH
        )

    for dx in (-1, 1):
        for dy in (-1, 1):
            pl.semaphore_signal(barrier, inc=1, device_id=shifted(dx, dy), device_id_type=MESH)

    stack[COLS - 1] = jnp.zeros((PITCH, ZC), F32)
    scale[...] = jnp.ones_like(scale)

    def put(post, step, x):
        for i in range(19):
            posts[step][PLACE[i], x + 1] = post[i]
        for p, i in enumerate(Y_UP):
            out_up[step, p, pl.ds(x, 1), :] = post[i][NY - 1 : NY, :]
        for p, i in enumerate(Y_DOWN):
            out_down[step, p, pl.ds(x, 1), :] = post[i][0:1, :]

    def halo(step):
        post = posts[step]
        inner = pl.ds(HALO0, NX)
        moves = [
            (post.at[pl.ds(0, 5), NX], post.at[pl.ds(0, 5), 0], (1, 0)),
            (post.at[pl.ds(5, 5), 1], post.at[pl.ds(5, 5), NX + 1], (-1, 0)),
            (out_up.at[step], in_up.at[step, :, inner, :], (0, 1)),
            (out_down.at[step], in_down.at[step, :, inner, :], (0, -1)),
        ]
        for c, (i, plane, dx, dy) in enumerate(CORNERS):
            moves.append((post.at[PLACE[i], plane], in_corner.at[step, c], (dx, dy)))
        return [
            pltpu.make_async_remote_copy(
                src_ref=src,
                dst_ref=dst,
                send_sem=halo_send.at[step, k],
                recv_sem=halo_recv.at[step, k],
                device_id=shifted(*to),
                device_id_type=MESH,
            )
            for k, (src, dst, to) in enumerate(moves)
        ]

    def land(step):
        for c, (i, plane, dx, dy) in enumerate(CORNERS):
            at = HALO0 - 1 if dx == 1 else HALO0 + NX
            if dy == 1:
                in_up[step, Y_UP.index(i), at : at + 1, :] = in_corner[step, c, NY - 1 : NY, :]
            else:
                in_down[step, Y_DOWN.index(i), at : at + 1, :] = in_corner[step, c, 0:1, :]

    loads[0].wait()
    loads[1].wait()

    @pl.loop(0, NX)
    def _(x):
        load_plane(x).wait()
        field = [pops[i, x] for i in range(19)]
        put(collide(field, rate[x], mask[x] > 0), 0, x)

    pl.semaphore_wait(barrier, (nx - 1) + (ny - 1) + 4)
    first = halo(0)
    for copy in first:
        copy.start()

    loads[2].wait()
    loads[3].wait()
    loads[4].wait()
    rows = stack.reshape(COLS * PITCH, ZC)
    gram[...] = jnp.zeros_like(gram)

    def tall(c, wide):
        return jnp.concatenate(
            [rows[pl.ds(c * wide + w, COLS, stride=PITCH), :] for w in range(wide)], axis=1
        )

    @pl.loop(0, ROWS // 32)
    def _(c):
        hi, lo = split(tall(c, 32))
        gram[:, 0:COLS] += dot(jnp.concatenate([hi, lo], axis=0), hi, 1, 1)

    low = jnp.concatenate([gram[COLS : 2 * COLS, :], jnp.zeros((ZC - COLS, ZC), F32)], axis=0)
    parts[...] = gram[0:COLS, :] + low[0:COLS] + jnp.transpose(low)[0:COLS]

    def to_owner(j):
        peer = lax.rem(mx + j, nx)
        chunk = lax.rem(peer, owners)
        return peer, pltpu.make_async_remote_copy(
            src_ref=parts.at[pl.ds(pl.multiple_of(chunk * 8, 8), 8)],
            dst_ref=recv_a.at[mx],
            send_sem=red_send.at[0],
            recv_sem=red_recv.at[0],
            device_id=(peer, my),
            device_id_type=MESH,
        )

    @pl.loop(1, nx)
    def _(j):
        peer, copy = to_owner(j)

        @pl.when(peer < owners)
        def _():
            copy.start()

    own = pl.ds(pl.multiple_of(lax.rem(mx, owners) * 8, 8), 8)
    recv_a[mx] = parts[own, :]

    for copy in first:
        copy.wait_recv()
    land(0)

    @pl.loop(0, NX)
    def _(x):
        field = arrive(post_a, in_up.at[0], in_down.at[0], x)
        put(collide(field, rate[x], mask[x] > 0), 1, x)

    second = halo(1)
    for copy in second:
        copy.start()

    def all_along(src, dst, k, axis):
        def copy(j):
            if axis == 0:
                peer = (lax.rem(mx + j, nx), my)
            else:
                peer = (mx, lax.rem(my + j, ny))
            return pltpu.make_async_remote_copy(
                src_ref=src,
                dst_ref=dst,
                send_sem=red_send.at[k],
                recv_sem=red_recv.at[k],
                device_id=peer,
                device_id_type=MESH,
            )

        return copy

    def start_all(copy, count):
        @pl.loop(1, count)
        def _(j):
            copy(j).start()

    def wait_for(ref, sem):
        pltpu.make_async_copy(ref, ref, sem).wait()

    def total(ref, count):
        value = ref[0]
        for j in range(1, count):
            value = value + ref[j]
        return value

    ring_b = all_along(send_b.at[0], recv_b.at[my], 1, 1)
    ring_c = all_along(send_b.at[1], recv_c.at[mx], 2, 0)

    @pl.when(mx < owners)
    def _():
        wait_for(recv_a.at[pl.ds(0, nx - 1)], red_recv.at[0])
        value = total(recv_a, nx)
        send_b[0] = value
        recv_b[my] = value
        start_all(ring_b, ny)

    for copy in second:
        copy.wait_recv()

    @pl.when(mx < owners)
    def _():
        wait_for(recv_b.at[pl.ds(0, ny - 1)], red_recv.at[1])
        value = total(recv_b, ny)
        send_b[1] = value
        recv_c[mx] = value
        start_all(ring_c, nx)

    land(1)

    @pl.loop(0, XC)
    def _(xc):
        sums = [None] * 3
        for half in range(2):
            x = 2 * xc + half
            field = arrive(post_b, in_up.at[1], in_down.at[1], x)
            for i in range(19):
                field_out[i, x] = field[i]
            fluid = mask[x] == 0
            for a, u in enumerate(flow(field)[1]):
                u = jnp.where(fluid, u, 0.0)
                sums[a] = u if half == 0 else sums[a] + u
        for a in range(3):
            vel[pl.ds(pl.multiple_of(a * XC * NY + xc * NY, NY), NY), :] = sums[a]

    fine = lax.broadcasted_iota(jnp.int32, (NZ, ZC), 0)
    pair = lax.broadcasted_iota(jnp.int32, (NZ, ZC), 1)
    pick = jnp.where(fine // 2 == pair, SPEED_SCALE / 8.0, 0.0).astype(F32)
    pooled[...] = dot(vel[...], pick, 1, 0, HIGHEST)
    coarse = pooled[pl.ds(0, ROWS, stride=2), :] + pooled[pl.ds(1, ROWS, stride=2), :]
    coarse_ref[...] = coarse
    stack[COLS - 1, 0:ROWS, :] = coarse

    tiles = ROWS // 8
    parted = coarse.reshape(tiles, 8, ZC)

    @pl.loop(0, COLS // 8)
    def _(k):
        for q in range(8):
            column = stack[k * 8 + q, 0:ROWS, :].reshape(tiles, 8, ZC)
            sums8[pl.ds(pl.multiple_of(k * 64 + q * 8, 8), 8), :] = jnp.sum(column * parted, axis=0)

    folded = sums8[pl.ds(0, COLS, stride=8), :]
    for q in range(1, 8):
        folded = folded + sums8[pl.ds(q, COLS, stride=8), :]
    folded = jnp.concatenate([folded, jnp.zeros((ZC - COLS, ZC), F32)], axis=0)
    last = dot(jnp.ones((8, ZC), F32), folded, 1, 1, HIGHEST)
    one = pl.ds(0, 1)
    vec_b[0] = last
    vec_in_a[mx] = last
    ring_d = all_along(vec_b.at[0, one], vec_in_a.at[mx, one], 3, 0)
    start_all(ring_d, nx)

    @pl.when(mx < owners)
    def _():
        wait_for(recv_c.at[pl.ds(0, owners - 1)], red_recv.at[2])

    @pl.when(mx >= owners)
    def _():
        wait_for(recv_c.at[pl.ds(0, owners)], red_recv.at[2])

    row = lax.broadcasted_iota(jnp.int32, (COLS, ZC), 0)
    lane = lax.broadcasted_iota(jnp.int32, (COLS, ZC), 1)
    scale[0:1, 0:RANK] = sv[...]
    srow = scale[0:1, :]
    scol = jnp.sum(jnp.where(row == lane, srow, 0.0), axis=1, keepdims=True)
    per_row = 1.0 / (all_rows(nx, ny))
    whole = jnp.concatenate([recv_c[c] for c in range(owners)], axis=0)
    whole = whole * (srow * scol) * per_row
    whole = jnp.where((row == COLS - 1) & (lane == COLS - 1), 1.0, whole)

    work[...] = whole
    inverse_ref[...] = (row == lane).astype(F32)

    def vec_total(ref, count):
        value = ref[0, 0:1, :]
        for j in range(1, count):
            value = value + ref[j, 0:1, :]
        return value

    half = owners // 2 - 1
    for b in range(half):
        factor_block(b, work, inverse_ref, upper_ref)

    wait_for(vec_in_a.at[pl.ds(0, nx - 1), one], red_recv.at[3])
    value = jnp.broadcast_to(vec_total(vec_in_a, nx), (8, ZC))
    vec_b[1] = value
    vec_in_b[my] = value
    ring_e = all_along(vec_b.at[1, one], vec_in_b.at[my, one], 4, 1)
    start_all(ring_e, ny)

    for b in range(half, owners):
        factor_block(b, work, inverse_ref, upper_ref)

    scaled = inverse_ref[...] * srow
    hi = scaled.astype(BF16).astype(F32)
    lo = scaled - hi
    none = jnp.zeros_like(hi)
    hi, lo = jnp.concatenate([hi, none], axis=1), jnp.concatenate([lo, none], axis=1)
    placed = hi + pltpu.roll(lo, COLS, axis=1) + pltpu.roll(hi, 2 * COLS, axis=1)
    left[...] = placed.astype(BF16)
    made = fresh.reshape(COLS * PITCH, ZC)

    @pl.loop(0, ROWS // 16)
    def _(c):
        hi, lo = split(tall(c, 16))
        result = dot(left[:, 0 : 3 * COLS], jnp.concatenate([hi, hi, lo], axis=0), 1, 0)
        for w in range(16):
            made[pl.ds(c * 16 + w, COLS, stride=PITCH), :] = result[:, w * ZC : (w + 1) * ZC]

    wait_for(vec_in_b.at[pl.ds(0, ny - 1), one], red_recv.at[4])
    border_ref[...] = jnp.broadcast_to(vec_total(vec_in_b, ny) * srow * per_row, (8, ZC))

    for copy in first + second:
        copy.wait_send()

    @pl.when(mx < owners)
    def _():
        wait_for(recv_a.at[pl.ds(0, owners - 1)], red_send.at[0])
        wait_for(recv_b.at[pl.ds(0, ny - 1)], red_send.at[1])
        wait_for(recv_a.at[pl.ds(0, nx - 1)], red_send.at[2])

    @pl.when(mx >= owners)
    def _():
        wait_for(recv_a.at[pl.ds(0, owners)], red_send.at[0])

    wait_for(vec_in_a.at[pl.ds(0, nx - 1), one], red_send.at[3])
    wait_for(vec_in_b.at[pl.ds(0, ny - 1), one], red_send.at[4])


def all_rows(nx, ny):
    return float(ROWS * ZC * nx * ny)


def finish_kernel(
    field_ref,
    fresh_ref,
    coarse_ref,
    inverse_ref,
    upper_ref,
    border_ref,
    pops_hbm,
    factor_ref,
    new_hbm,
    column,
    newest,
    sem,
):
    done = pl.ds(0, COLS - 1)
    copies = [
        pltpu.make_async_copy(fresh_ref.at[done, pl.ds(0, ROWS)], new_hbm.at[done], sem.at[0]),
        pltpu.make_async_copy(field_ref, pops_hbm, sem.at[1]),
        pltpu.make_async_copy(newest, new_hbm.at[COLS - 1], sem.at[2]),
    ]
    copies[0].start()
    copies[1].start()

    row = lax.broadcasted_iota(jnp.int32, (COLS, ZC), 0)
    lane = lax.broadcasted_iota(jnp.int32, (COLS, ZC), 1)
    inverse = inverse_ref[...]
    border = border_ref[...]
    lane8 = lax.broadcasted_iota(jnp.int32, (8, ZC), 1)
    old = jnp.where(lane8 < COLS - 1, border, 0.0)
    lcol = dot(inverse, jnp.concatenate([old] * (ZC // 8), axis=0), 1, 1, HIGHEST)
    lcol = jnp.where(row < COLS - 1, lcol, 0.0)
    column[...] = lcol
    square = border[0:1, COLS - 1 : COLS] - jnp.sum(lcol * lcol, axis=0, keepdims=True)
    inv = lax.rsqrt(square)
    end = jnp.where(row == COLS - 1, square * inv, lcol)
    factor_ref[...] = jnp.where(lane == COLS - 1, end, upper_ref[...])[:, 0:COLS]

    def minus(k, value):
        for q in range(8):
            i = k * 8 + q
            value = value - column[pl.ds(i, 1), :] * fresh_ref[i, 0:ROWS, :]
        return value

    newest[...] = lax.fori_loop(0, COLS // 8, minus, coarse_ref[...]) * inv
    copies[2].start()
    for copy in copies:
        copy.wait()


def on_device(nx, ny, pops, rate, mask, sv, basis, snaps):
    sv = sv.reshape(1, RANK)
    basis = basis.reshape(RANK, ROWS, ZC)
    snaps = snaps.reshape(OLD, ROWS, ZC)
    given = (pops, rate, mask, sv, basis, snaps)
    given = [pltpu.with_memory_space_constraint(x, pltpu.HBM) for x in given]
    far = pl.BlockSpec(memory_space=pltpu.HBM)
    here = pl.BlockSpec(memory_space=pltpu.VMEM)
    owners = COLS // 8

    def f32(*shape):
        return jax.ShapeDtypeStruct(shape, F32)

    def vmem(*shape):
        return pltpu.VMEM(shape, F32)

    dma = pltpu.SemaphoreType.DMA
    field, fresh, coarse, inverse, upper, border = pl.pallas_call(
        functools.partial(main_kernel, nx, ny),
        out_shape=(
            f32(19, NX, NY, NZ),
            f32(COLS, PITCH, ZC),
            f32(ROWS, ZC),
            f32(COLS, ZC),
            f32(COLS, ZC),
            f32(8, ZC),
        ),
        in_specs=[far] * 6,
        out_specs=(here,) * 6,
        scratch_shapes=[
            vmem(19, NX, NY, NZ),
            vmem(NX, NY, NZ),
            pltpu.VMEM((NX, NY, NZ), jnp.int32),
            vmem(COLS, PITCH, ZC),
            vmem(19, NX + 2, NY, NZ),
            vmem(19, NX + 2, NY, NZ),
            vmem(2, 5, NX, NZ),
            vmem(2, 5, NX, NZ),
            vmem(2, 5, NX + 16, NZ),
            vmem(2, 5, NX + 16, NZ),
            vmem(2, 4, NY, NZ),
            vmem(3 * XC * NY, NZ),
            vmem(3 * XC * NY, ZC),
            vmem(2 * COLS, ZC),
            vmem(COLS, ZC),
            vmem(nx, 8, ZC),
            vmem(2, 8, ZC),
            vmem(ny, 8, ZC),
            vmem(owners, 8, ZC),
            vmem(8 * COLS, ZC),
            vmem(2, 8, ZC),
            vmem(nx, 8, ZC),
            vmem(ny, 8, ZC),
            vmem(1, RANK),
            vmem(8, ZC),
            vmem(COLS, ZC),
            pltpu.VMEM((COLS, 2 * ZC), BF16),
            dma((NX,)),
            dma((5,)),
            dma((2, 8)),
            dma((2, 8)),
            dma((5,)),
            dma((5,)),
        ],
        compiler_params=pltpu.CompilerParams(
            collective_id=0, has_side_effects=True, vmem_limit_bytes=40 * 2**20
        ),
        name="substeps",
    )(*given)
    out, factor, new = pl.pallas_call(
        finish_kernel,
        out_shape=(f32(19, NX, NY, NZ), f32(COLS, COLS), f32(COLS, ROWS, ZC)),
        in_specs=[here] * 6,
        out_specs=(far, here, far),
        scratch_shapes=[vmem(COLS, ZC), vmem(ROWS, ZC), dma((3,))],
        compiler_params=pltpu.CompilerParams(vmem_limit_bytes=16 * 2**20),
        name="finish",
    )(field, fresh, coarse, inverse, upper, border)
    return out, factor, new.reshape(COLS, 3, XC, YC, ZC)


def solution(mesh):
    return jax.shard_map(
        functools.partial(on_device, mesh.shape["gx"], mesh.shape["gy"]),
        mesh=mesh,
        in_specs=(
            P(None, "gx", "gy", None),
            P("gx", "gy", None),
            P("gx", "gy", None),
            P(),
            P(None, None, "gx", "gy", None),
            P(None, None, "gx", "gy", None),
        ),
        out_specs=(P(None, "gx", "gy", None), P(), P(None, None, "gx", "gy", None)),
        check_vma=False,
    )
```

```python
import functools

import jax
import jax.numpy as jnp
from jax import lax
from jax.experimental import pallas as pl
from jax.experimental.pallas import tpu as pltpu
from jax.sharding import PartitionSpec as P

MESH = pl.DeviceIdType.MESH
HIGHEST = lax.Precision.HIGHEST
F32 = jnp.float32
BF16 = jnp.bfloat16

VELOCITY = [
    (0, 0, 0),
    (1, 0, 0),
    (-1, 0, 0),
    (0, 1, 0),
    (0, -1, 0),
    (0, 0, 1),
    (0, 0, -1),
    (1, 1, 0),
    (-1, -1, 0),
    (1, -1, 0),
    (-1, 1, 0),
    (1, 0, 1),
    (-1, 0, -1),
    (1, 0, -1),
    (-1, 0, 1),
    (0, 1, 1),
    (0, -1, -1),
    (0, 1, -1),
    (0, -1, 1),
]
SPEED_SCALE = 10.0

ORDER = [1, 7, 9, 11, 13, 2, 8, 10, 12, 14, 0, 3, 4, 5, 6, 15, 16, 17, 18]
PLACE = [ORDER.index(i) for i in range(19)]
Y_UP = [3, 7, 10, 15, 17]
Y_DOWN = [4, 8, 9, 16, 18]
CORNERS = [(7, 16, 1, 1), (8, 1, -1, -1), (9, 16, 1, -1), (10, 1, -1, 1)]

NX, NY, NZ = 16, 8, 256
XC, YC, ZC = 8, 4, 128
COLS, RANK, OLD = 80, 64, 15
ROWS = 3 * XC * YC
PITCH = ROWS + 8
HALO0 = 8


def flow(field):
    plus = [field[i] + field[i + 1] for i in range(1, 19, 2)]
    diff = [field[i] - field[i + 1] for i in range(1, 19, 2)]
    rho = field[0]
    for s in plus:
        rho = rho + s
    comps = []
    for axis in range(3):
        total = None
        for p, d in enumerate(diff):
            c = VELOCITY[2 * p + 1][axis]
            if c:
                total = d if total is None else (total + d if c > 0 else total - d)
        comps.append(total)
    inv = 1.0 / rho
    return rho, [c * inv for c in comps]


def collide(field, rate, solid):
    rho, vel = flow(field)
    tri = [3.0 * u for u in vel]
    base = 1.0 - 1.5 * (vel[0] * vel[0] + vel[1] * vel[1] + vel[2] * vel[2])
    post = [None] * 19
    face = rho * (1.0 / 18.0)
    edge = rho * (1.0 / 36.0)
    rest = rho * (1.0 / 3.0) * base
    post[0] = jnp.where(solid, field[0], field[0] + rate * (rest - field[0]))
    for i in range(1, 19, 2):
        along = None
        for axis in range(3):
            c = VELOCITY[i][axis]
            if c:
                along = (
                    tri[axis]
                    if along is None
                    else (along + tri[axis] if c > 0 else along - tri[axis])
                )
        weight = face if i < 7 else edge
        even = weight * (base + 0.5 * (along * along))
        odd = weight * along
        fp, fm = field[i], field[i + 1]
        post[i] = jnp.where(solid, fm, fp + rate * ((even + odd) - fp))
        post[i + 1] = jnp.where(solid, fp, fm + rate * ((even - odd) - fm))
    return post


def arrive(post_ref, up_ref, down_ref, x):
    row = lax.broadcasted_iota(jnp.int32, (NY, NZ), 0)
    field = []
    for i, (cx, cy, cz) in enumerate(VELOCITY):
        v = post_ref[PLACE[i], x + 1 - cx]
        if cy == 1:
            halo = up_ref[Y_UP.index(i), pl.ds(x + HALO0 - cx, 1), :]
            v = jnp.where(row == 0, halo, pltpu.roll(v, 1, axis=0))
        elif cy == -1:
            halo = down_ref[Y_DOWN.index(i), pl.ds(x + HALO0 - cx, 1), :]
            v = jnp.where(row == NY - 1, halo, pltpu.roll(v, NY - 1, axis=0))
        if cz == 1:
            v = pltpu.roll(v, 1, axis=1)
        elif cz == -1:
            v = pltpu.roll(v, NZ - 1, axis=1)
        field.append(v)
    return field


def split(x):
    hi = x.astype(BF16)
    lo = (x - hi.astype(F32)).astype(BF16)
    return hi, lo


def dot(a, b, ca, cb, precision=None):
    return lax.dot_general(
        a, b, (((ca,), (cb,)), ((), ())), precision=precision, preferred_element_type=F32
    )


def split3(x):
    hi = x.astype(BF16).astype(F32)
    mid = (x - hi).astype(BF16).astype(F32)
    return hi, mid, x - hi - mid


def outer8(r, t):
    h, m, l = split3(jnp.concatenate([r, t], axis=1))
    rh, rm, rl = h[:, 0:ZC], m[:, 0:ZC], l[:, 0:ZC]
    a = jnp.concatenate([rh, rh, rh, rm, rm, rl], axis=0).astype(BF16)
    b = jnp.concatenate([h, m, l, h, m, h], axis=0).astype(BF16)
    return dot(a, b, 0, 0)


def eliminate(rows, extra, first):
    d = [
        [jnp.broadcast_to(rows[i][:, first + j : first + j + 1], (1, ZC)) for j in range(i + 1)]
        for i in range(8)
    ]
    r, t = list(rows), list(extra)
    for j in range(8):
        inv = lax.rsqrt(d[j][j])
        r[j] = r[j] * inv
        t[j] = t[j] * inv
        col = [None if i <= j else d[i][j] * inv for i in range(8)]
        for i in range(j + 1, 8):
            for k in range(j + 1, i + 1):
                d[i][k] = d[i][k] - col[i] * col[k]
            r[i] = r[i] - col[i] * r[j]
            t[i] = t[i] - col[i] * t[j]
    return jnp.concatenate(r, axis=0), jnp.concatenate(t, axis=0)


def factor_block(b, work, inverse, upper):
    row8 = lax.broadcasted_iota(jnp.int32, (8, ZC), 0)
    lane8 = lax.broadcasted_iota(jnp.int32, (8, ZC), 1)
    o = 8 * b
    r, t = eliminate(
        [work[o + i : o + i + 1, :] for i in range(8)],
        [inverse[o + i : o + i + 1, :] for i in range(8)],
        o,
    )
    r = jnp.where(lane8 >= row8 + o, r, 0.0)
    upper[o : o + 8, :] = r
    inverse[o : o + 8, :] = t
    if o + 8 < COLS:
        change = outer8(r, t)
        work[o + 8 : COLS, :] = work[o + 8 : COLS, :] - change[o + 8 : COLS, 0:ZC]
        inverse[o + 8 : COLS, :] = inverse[o + 8 : COLS, :] - change[o + 8 : COLS, ZC:]


def main_kernel(
    nx,
    ny,
    pops_hbm,
    rate_hbm,
    mask_hbm,
    sv_hbm,
    basis_hbm,
    snaps_hbm,
    field_out,
    fresh,
    coarse_ref,
    inverse_ref,
    upper_ref,
    border_ref,
    pops,
    rate,
    mask,
    stack,
    post_a,
    post_b,
    out_up,
    out_down,
    in_up,
    in_down,
    vel,
    pooled,
    gram,
    parts,
    recv_a,
    send_b,
    recv_b,
    recv_c,
    sums8,
    vec_b,
    vec_in_a,
    vec_in_b,
    sv,
    scale,
    work,
    left,
    plane_sem,
    load_sem,
    halo_send,
    halo_recv,
    red_send,
    red_recv,
):
    mx, my = lax.axis_index("gx"), lax.axis_index("gy")
    owners = COLS // 8
    posts = (post_a, post_b)

    def shifted(dx, dy):
        return (lax.rem(mx + (dx + nx), nx), lax.rem(my + (dy + ny), ny))

    def load_planes(g):
        part = pl.ds(4 * g, 4)
        return pltpu.make_async_copy(pops_hbm.at[:, part], pops.at[:, part], plane_sem.at[g])

    loads = [
        pltpu.make_async_copy(rate_hbm, rate, load_sem.at[0]),
        pltpu.make_async_copy(mask_hbm, mask, load_sem.at[1]),
        pltpu.make_async_copy(basis_hbm, stack.at[pl.ds(0, RANK), pl.ds(0, ROWS)], load_sem.at[2]),
        pltpu.make_async_copy(snaps_hbm, stack.at[pl.ds(RANK, OLD), pl.ds(0, ROWS)], load_sem.at[3]),
        pltpu.make_async_copy(sv_hbm, sv, load_sem.at[4]),
    ]
    for g in range(NX // 4):
        load_planes(g).start()
    loads[0].start()
    loads[1].start()

    barrier = pltpu.get_barrier_semaphore()

    def greet(to):
        pl.semaphore_signal(barrier, inc=1, device_id=to, device_id_type=MESH)

    for dx in (-1, 1):
        for dy in (-1, 1):
            greet(shifted(dx, dy))

    @pl.loop(0, nx - 1)
    def _(j):
        greet((lax.rem(mx + nx // 2 + j + lax.div(j, nx // 2), nx), my))

    @pl.loop(0, ny - 1)
    def _(j):
        greet((mx, lax.rem(my + ny // 2 + j + lax.div(j, ny // 2), ny)))

    loads[2].start()
    loads[3].start()
    loads[4].start()

    stack[COLS - 1] = jnp.zeros((PITCH, ZC), F32)
    scale[...] = jnp.ones_like(scale)

    def put(post, step, x):
        for i in range(19):
            posts[step][PLACE[i], x + 1] = post[i]
        for p, i in enumerate(Y_UP):
            out_up[step, p, pl.ds(x, 1), :] = post[i][NY - 1 : NY, :]
        for p, i in enumerate(Y_DOWN):
            out_down[step, p, pl.ds(x, 1), :] = post[i][0:1, :]

    def halo(step):
        post = posts[step]
        moves = []
        for i, plane, dx, dy in CORNERS:
            row = NY - 1 if dy == 1 else 0
            src = post.at[PLACE[i], plane, pl.ds(row, 1), :]
            at = pl.ds(HALO0 - 1 if dx == 1 else HALO0 + NX, 1)
            if dy == 1:
                dst = in_up.at[step, Y_UP.index(i), at, :]
            else:
                dst = in_down.at[step, Y_DOWN.index(i), at, :]
            moves.append((src, dst, (dx, dy)))
        moves.append((post.at[pl.ds(0, 5), NX], post.at[pl.ds(0, 5), 0], (1, 0)))
        moves.append((post.at[pl.ds(5, 5), 1], post.at[pl.ds(5, 5), NX + 1], (-1, 0)))
        for first in (0, NX // 2):
            src, dst = pl.ds(first, NX // 2), pl.ds(HALO0 + first, NX // 2)
            moves.append((out_up.at[step, :, src, :], in_up.at[step, :, dst, :], (0, 1)))
            moves.append((out_down.at[step, :, src, :], in_down.at[step, :, dst, :], (0, -1)))
        return [
            pltpu.make_async_remote_copy(
                src_ref=src,
                dst_ref=dst,
                send_sem=halo_send.at[step, k],
                recv_sem=halo_recv.at[step, k],
                device_id=shifted(*to),
                device_id_type=MESH,
            )
            for k, (src, dst, to) in enumerate(moves)
        ]

    loads[0].wait()
    loads[1].wait()
    for g in range(NX // 4):
        load_planes(g).wait()

        @pl.loop(4 * g, 4 * g + 4)
        def _(x):
            field = [pops[i, x] for i in range(19)]
            put(collide(field, rate[x], mask[x] > 0), 0, x)

    pl.semaphore_wait(barrier, (nx - 1) + (ny - 1) + 4)
    first = halo(0)
    for copy in first:
        copy.start()

    loads[2].wait()
    loads[3].wait()
    loads[4].wait()
    rows = stack.reshape(COLS * PITCH, ZC)
    gram[...] = jnp.zeros_like(gram)

    def tall(c, wide):
        return jnp.concatenate(
            [rows[pl.ds(c * wide + w, COLS, stride=PITCH), :] for w in range(wide)], axis=1
        )

    @pl.loop(0, ROWS // 32)
    def _(c):
        hi, lo = split(tall(c, 32))
        gram[:, 0:COLS] += dot(jnp.concatenate([hi, lo], axis=0), hi, 1, 1)

    low = jnp.concatenate([gram[COLS : 2 * COLS, :], jnp.zeros((ZC - COLS, ZC), F32)], axis=0)
    parts[...] = gram[0:COLS, :] + low[0:COLS] + jnp.transpose(low)[0:COLS]

    def to_owner(j):
        peer = lax.rem(mx + j, nx)
        chunk = lax.rem(peer, owners)
        return peer, pltpu.make_async_remote_copy(
            src_ref=parts.at[pl.ds(pl.multiple_of(chunk * 8, 8), 8)],
            dst_ref=recv_a.at[mx],
            send_sem=red_send.at[0],
            recv_sem=red_recv.at[0],
            device_id=(peer, my),
            device_id_type=MESH,
        )

    @pl.loop(1, nx)
    def _(j):
        peer, copy = to_owner(j)

        @pl.when(peer < owners)
        def _():
            copy.start()

    own = pl.ds(pl.multiple_of(lax.rem(mx, owners) * 8, 8), 8)
    recv_a[mx] = parts[own, :]

    for copy in first:
        copy.wait_recv()
    second = halo(1)

    @pl.loop(0, NX)
    def _(k):
        x = lax.rem(k + (NX - 1), NX)
        field = arrive(post_a, in_up.at[0], in_down.at[0], x)
        put(collide(field, rate[x], mask[x] > 0), 1, x)

        @pl.when(k == 1)
        def _():
            for copy in second[0:6]:
                copy.start()

        @pl.when(k == NX // 2)
        def _():
            for copy in second[6:8]:
                copy.start()

    for copy in second[8:10]:
        copy.start()

    def all_along(src, dst, k, axis):
        def copy(j):
            if axis == 0:
                peer = (lax.rem(mx + j, nx), my)
            else:
                peer = (mx, lax.rem(my + j, ny))
            return pltpu.make_async_remote_copy(
                src_ref=src,
                dst_ref=dst,
                send_sem=red_send.at[k],
                recv_sem=red_recv.at[k],
                device_id=peer,
                device_id_type=MESH,
            )

        return copy

    def start_all(copy, count):
        @pl.loop(1, count)
        def _(j):
            copy(j).start()

    def wait_for(ref, sem):
        pltpu.make_async_copy(ref, ref, sem).wait()

    def total(ref, count):
        value = ref[0]
        for j in range(1, count):
            value = value + ref[j]
        return value

    ring_b = all_along(send_b.at[0], recv_b.at[my], 1, 1)
    ring_c = all_along(send_b.at[1], recv_c.at[mx], 2, 0)

    @pl.when(mx < owners)
    def _():
        wait_for(recv_a.at[pl.ds(0, nx - 1)], red_recv.at[0])
        value = total(recv_a, nx)
        send_b[0] = value
        recv_b[my] = value
        start_all(ring_b, ny)

    for copy in second:
        copy.wait_recv()

    @pl.when(mx < owners)
    def _():
        wait_for(recv_b.at[pl.ds(0, ny - 1)], red_recv.at[1])
        value = total(recv_b, ny)
        send_b[1] = value
        recv_c[mx] = value
        start_all(ring_c, nx)


    @pl.loop(0, XC)
    def _(xc):
        sums = [None] * 3
        for half in range(2):
            x = 2 * xc + half
            field = arrive(post_b, in_up.at[1], in_down.at[1], x)
            for i in range(19):
                field_out[i, x] = field[i]
            fluid = mask[x] == 0
            for a, u in enumerate(flow(field)[1]):
                u = jnp.where(fluid, u, 0.0)
                sums[a] = u if half == 0 else sums[a] + u
        for a in range(3):
            vel[pl.ds(pl.multiple_of(a * XC * NY + xc * NY, NY), NY), :] = sums[a]

    fine = lax.broadcasted_iota(jnp.int32, (NZ, ZC), 0)
    pair = lax.broadcasted_iota(jnp.int32, (NZ, ZC), 1)
    pick = jnp.where(fine // 2 == pair, SPEED_SCALE / 8.0, 0.0).astype(F32)
    pooled[...] = dot(vel[...], pick, 1, 0, HIGHEST)
    coarse = pooled[pl.ds(0, ROWS, stride=2), :] + pooled[pl.ds(1, ROWS, stride=2), :]
    coarse_ref[...] = coarse
    stack[COLS - 1, 0:ROWS, :] = coarse

    tiles = ROWS // 8
    parted = coarse.reshape(tiles, 8, ZC)

    @pl.loop(0, COLS // 8)
    def _(k):
        for q in range(8):
            column = stack[k * 8 + q, 0:ROWS, :].reshape(tiles, 8, ZC)
            sums8[pl.ds(pl.multiple_of(k * 64 + q * 8, 8), 8), :] = jnp.sum(column * parted, axis=0)

    folded = sums8[pl.ds(0, COLS, stride=8), :]
    for q in range(1, 8):
        folded = folded + sums8[pl.ds(q, COLS, stride=8), :]
    folded = jnp.concatenate([folded, jnp.zeros((ZC - COLS, ZC), F32)], axis=0)
    last = dot(jnp.ones((8, ZC), F32), folded, 1, 1, HIGHEST)
    one = pl.ds(0, 1)
    vec_b[0] = last
    vec_in_a[mx] = last
    ring_d = all_along(vec_b.at[0, one], vec_in_a.at[mx, one], 3, 0)
    start_all(ring_d, nx)

    @pl.when(mx < owners)
    def _():
        wait_for(recv_c.at[pl.ds(0, owners - 1)], red_recv.at[2])

    @pl.when(mx >= owners)
    def _():
        wait_for(recv_c.at[pl.ds(0, owners)], red_recv.at[2])

    row = lax.broadcasted_iota(jnp.int32, (COLS, ZC), 0)
    lane = lax.broadcasted_iota(jnp.int32, (COLS, ZC), 1)
    scale[0:1, 0:RANK] = sv[...]
    srow = scale[0:1, :]
    scol = jnp.sum(jnp.where(row == lane, srow, 0.0), axis=1, keepdims=True)
    per_row = 1.0 / (all_rows(nx, ny))
    whole = jnp.concatenate([recv_c[c] for c in range(owners)], axis=0)
    whole = whole * (srow * scol) * per_row
    whole = jnp.where((row == COLS - 1) & (lane == COLS - 1), 1.0, whole)

    work[...] = whole
    inverse_ref[...] = (row == lane).astype(F32)

    def vec_total(ref, count):
        value = ref[0, 0:1, :]
        for j in range(1, count):
            value = value + ref[j, 0:1, :]
        return value

    half = owners // 2 - 1
    for b in range(half):
        factor_block(b, work, inverse_ref, upper_ref)

    wait_for(vec_in_a.at[pl.ds(0, nx - 1), one], red_recv.at[3])
    value = jnp.broadcast_to(vec_total(vec_in_a, nx), (8, ZC))
    vec_b[1] = value
    vec_in_b[my] = value
    ring_e = all_along(vec_b.at[1, one], vec_in_b.at[my, one], 4, 1)
    start_all(ring_e, ny)

    for b in range(half, owners):
        factor_block(b, work, inverse_ref, upper_ref)

    scaled = inverse_ref[...] * srow
    hi = scaled.astype(BF16).astype(F32)
    lo = scaled - hi
    none = jnp.zeros_like(hi)
    hi, lo = jnp.concatenate([hi, none], axis=1), jnp.concatenate([lo, none], axis=1)
    placed = hi + pltpu.roll(lo, COLS, axis=1) + pltpu.roll(hi, 2 * COLS, axis=1)
    left[...] = placed.astype(BF16)
    made = fresh.reshape(COLS * PITCH, ZC)

    @pl.loop(0, ROWS // 16)
    def _(c):
        hi, lo = split(tall(c, 16))
        result = dot(left[:, 0 : 3 * COLS], jnp.concatenate([hi, hi, lo], axis=0), 1, 0)
        for w in range(16):
            made[pl.ds(c * 16 + w, COLS, stride=PITCH), :] = result[:, w * ZC : (w + 1) * ZC]

    wait_for(vec_in_b.at[pl.ds(0, ny - 1), one], red_recv.at[4])
    border_ref[...] = jnp.broadcast_to(vec_total(vec_in_b, ny) * srow * per_row, (8, ZC))

    for copy in first + second:
        copy.wait_send()

    @pl.when(mx < owners)
    def _():
        wait_for(recv_a.at[pl.ds(0, owners - 1)], red_send.at[0])
        wait_for(recv_b.at[pl.ds(0, ny - 1)], red_send.at[1])
        wait_for(recv_a.at[pl.ds(0, nx - 1)], red_send.at[2])

    @pl.when(mx >= owners)
    def _():
        wait_for(recv_a.at[pl.ds(0, owners)], red_send.at[0])

    wait_for(vec_in_a.at[pl.ds(0, nx - 1), one], red_send.at[3])
    wait_for(vec_in_b.at[pl.ds(0, ny - 1), one], red_send.at[4])


def all_rows(nx, ny):
    return float(ROWS * ZC * nx * ny)


def finish_kernel(
    field_ref,
    fresh_ref,
    coarse_ref,
    inverse_ref,
    upper_ref,
    border_ref,
    pops_hbm,
    factor_ref,
    new_hbm,
    column,
    newest,
    sem,
):
    done = pl.ds(0, COLS - 1)
    copies = [
        pltpu.make_async_copy(fresh_ref.at[done, pl.ds(0, ROWS)], new_hbm.at[done], sem.at[0]),
        pltpu.make_async_copy(field_ref, pops_hbm, sem.at[1]),
        pltpu.make_async_copy(newest, new_hbm.at[COLS - 1], sem.at[2]),
    ]
    copies[0].start()
    copies[1].start()

    row = lax.broadcasted_iota(jnp.int32, (COLS, ZC), 0)
    lane = lax.broadcasted_iota(jnp.int32, (COLS, ZC), 1)
    inverse = inverse_ref[...]
    border = border_ref[...]
    lane8 = lax.broadcasted_iota(jnp.int32, (8, ZC), 1)
    old = jnp.where(lane8 < COLS - 1, border, 0.0)
    lcol = dot(inverse, jnp.concatenate([old] * (ZC // 8), axis=0), 1, 1, HIGHEST)
    lcol = jnp.where(row < COLS - 1, lcol, 0.0)
    column[...] = lcol
    square = border[0:1, COLS - 1 : COLS] - jnp.sum(lcol * lcol, axis=0, keepdims=True)
    inv = lax.rsqrt(square)
    end = jnp.where(row == COLS - 1, square * inv, lcol)
    factor_ref[...] = jnp.where(lane == COLS - 1, end, upper_ref[...])[:, 0:COLS]

    def minus(k, value):
        for q in range(8):
            i = k * 8 + q
            value = value - column[pl.ds(i, 1), :] * fresh_ref[i, 0:ROWS, :]
        return value

    newest[...] = lax.fori_loop(0, COLS // 8, minus, coarse_ref[...]) * inv
    copies[2].start()
    for copy in copies:
        copy.wait()


def on_device(nx, ny, pops, rate, mask, sv, basis, snaps):
    sv = sv.reshape(1, RANK)
    basis = basis.reshape(RANK, ROWS, ZC)
    snaps = snaps.reshape(OLD, ROWS, ZC)
    given = (pops, rate, mask, sv, basis, snaps)
    given = [pltpu.with_memory_space_constraint(x, pltpu.HBM) for x in given]
    far = pl.BlockSpec(memory_space=pltpu.HBM)
    here = pl.BlockSpec(memory_space=pltpu.VMEM)
    owners = COLS // 8

    def f32(*shape):
        return jax.ShapeDtypeStruct(shape, F32)

    def vmem(*shape):
        return pltpu.VMEM(shape, F32)

    dma = pltpu.SemaphoreType.DMA
    field, fresh, coarse, inverse, upper, border = pl.pallas_call(
        functools.partial(main_kernel, nx, ny),
        out_shape=(
            f32(19, NX, NY, NZ),
            f32(COLS, PITCH, ZC),
            f32(ROWS, ZC),
            f32(COLS, ZC),
            f32(COLS, ZC),
            f32(8, ZC),
        ),
        in_specs=[far] * 6,
        out_specs=(here,) * 6,
        scratch_shapes=[
            vmem(19, NX, NY, NZ),
            vmem(NX, NY, NZ),
            pltpu.VMEM((NX, NY, NZ), jnp.int32),
            vmem(COLS, PITCH, ZC),
            vmem(19, NX + 2, NY, NZ),
            vmem(19, NX + 2, NY, NZ),
            vmem(2, 5, NX, NZ),
            vmem(2, 5, NX, NZ),
            vmem(2, 5, NX + 16, NZ),
            vmem(2, 5, NX + 16, NZ),
            vmem(3 * XC * NY, NZ),
            vmem(3 * XC * NY, ZC),
            vmem(2 * COLS, ZC),
            vmem(COLS, ZC),
            vmem(nx, 8, ZC),
            vmem(2, 8, ZC),
            vmem(ny, 8, ZC),
            vmem(owners, 8, ZC),
            vmem(8 * COLS, ZC),
            vmem(2, 8, ZC),
            vmem(nx, 8, ZC),
            vmem(ny, 8, ZC),
            vmem(1, RANK),
            vmem(8, ZC),
            vmem(COLS, ZC),
            pltpu.VMEM((COLS, 2 * ZC), BF16),
            dma((NX // 4,)),
            dma((5,)),
            dma((2, 10)),
            dma((2, 10)),
            dma((5,)),
            dma((5,)),
        ],
        compiler_params=pltpu.CompilerParams(
            collective_id=0, has_side_effects=True, vmem_limit_bytes=40 * 2**20
        ),
        name="substeps",
    )(*given)
    out, factor, new = pl.pallas_call(
        finish_kernel,
        out_shape=(f32(19, NX, NY, NZ), f32(COLS, COLS), f32(COLS, ROWS, ZC)),
        in_specs=[here] * 6,
        out_specs=(far, here, far),
        scratch_shapes=[vmem(COLS, ZC), vmem(ROWS, ZC), dma((3,))],
        compiler_params=pltpu.CompilerParams(vmem_limit_bytes=16 * 2**20),
        name="finish",
    )(field, fresh, coarse, inverse, upper, border)
    return out, factor, new.reshape(COLS, 3, XC, YC, ZC)


def solution(mesh):
    return jax.shard_map(
        functools.partial(on_device, mesh.shape["gx"], mesh.shape["gy"]),
        mesh=mesh,
        in_specs=(
            P(None, "gx", "gy", None),
            P("gx", "gy", None),
            P("gx", "gy", None),
            P(),
            P(None, None, "gx", "gy", None),
            P(None, None, "gx", "gy", None),
        ),
        out_specs=(P(None, "gx", "gy", None), P(), P(None, None, "gx", "gy", None)),
        check_vma=False,
    )
```

```python
import functools

import jax
import jax.numpy as jnp
from jax import lax
from jax.experimental import pallas as pl
from jax.experimental.pallas import tpu as pltpu
from jax.sharding import PartitionSpec as P

MESH = pl.DeviceIdType.MESH
HIGHEST = lax.Precision.HIGHEST
F32 = jnp.float32
BF16 = jnp.bfloat16

VELOCITY = [
    (0, 0, 0),
    (1, 0, 0),
    (-1, 0, 0),
    (0, 1, 0),
    (0, -1, 0),
    (0, 0, 1),
    (0, 0, -1),
    (1, 1, 0),
    (-1, -1, 0),
    (1, -1, 0),
    (-1, 1, 0),
    (1, 0, 1),
    (-1, 0, -1),
    (1, 0, -1),
    (-1, 0, 1),
    (0, 1, 1),
    (0, -1, -1),
    (0, 1, -1),
    (0, -1, 1),
]
SPEED_SCALE = 10.0

ORDER = [1, 7, 9, 11, 13, 2, 8, 10, 12, 14, 0, 3, 4, 5, 6, 15, 16, 17, 18]
PLACE = [ORDER.index(i) for i in range(19)]
Y_UP = [3, 7, 10, 15, 17]
Y_DOWN = [4, 8, 9, 16, 18]
CORNERS = [(7, 16, 1, 1), (8, 1, -1, -1), (9, 16, 1, -1), (10, 1, -1, 1)]

NX, NY, NZ = 16, 8, 256
XC, YC, ZC = 8, 4, 128
COLS, RANK, OLD = 80, 64, 15
ROWS = 3 * XC * YC
PITCH = ROWS + 8
HALO0 = 8


def flow(field):
    plus = [field[i] + field[i + 1] for i in range(1, 19, 2)]
    diff = [field[i] - field[i + 1] for i in range(1, 19, 2)]
    rho = field[0]
    for s in plus:
        rho = rho + s
    comps = []
    for axis in range(3):
        total = None
        for p, d in enumerate(diff):
            c = VELOCITY[2 * p + 1][axis]
            if c:
                total = d if total is None else (total + d if c > 0 else total - d)
        comps.append(total)
    inv = 1.0 / rho
    return rho, [c * inv for c in comps]


def collide(field, rate, solid):
    rho, vel = flow(field)
    tri = [3.0 * u for u in vel]
    base = 1.0 - 1.5 * (vel[0] * vel[0] + vel[1] * vel[1] + vel[2] * vel[2])
    post = [None] * 19
    face = rho * (1.0 / 18.0)
    edge = rho * (1.0 / 36.0)
    rest = rho * (1.0 / 3.0) * base
    post[0] = jnp.where(solid, field[0], field[0] + rate * (rest - field[0]))
    for i in range(1, 19, 2):
        along = None
        for axis in range(3):
            c = VELOCITY[i][axis]
            if c:
                along = (
                    tri[axis]
                    if along is None
                    else (along + tri[axis] if c > 0 else along - tri[axis])
                )
        weight = face if i < 7 else edge
        even = weight * (base + 0.5 * (along * along))
        odd = weight * along
        fp, fm = field[i], field[i + 1]
        post[i] = jnp.where(solid, fm, fp + rate * ((even + odd) - fp))
        post[i + 1] = jnp.where(solid, fp, fm + rate * ((even - odd) - fm))
    return post


def arrive(post_ref, up_ref, down_ref, x):
    row = lax.broadcasted_iota(jnp.int32, (NY, NZ), 0)
    field = []
    for i, (cx, cy, cz) in enumerate(VELOCITY):
        v = post_ref[PLACE[i], x + 1 - cx]
        if cy == 1:
            halo = up_ref[Y_UP.index(i), pl.ds(x + HALO0 - cx, 1), :]
            v = jnp.where(row == 0, halo, pltpu.roll(v, 1, axis=0))
        elif cy == -1:
            halo = down_ref[Y_DOWN.index(i), pl.ds(x + HALO0 - cx, 1), :]
            v = jnp.where(row == NY - 1, halo, pltpu.roll(v, NY - 1, axis=0))
        if cz == 1:
            v = pltpu.roll(v, 1, axis=1)
        elif cz == -1:
            v = pltpu.roll(v, NZ - 1, axis=1)
        field.append(v)
    return field


def arrive_face(post_ref, up_ref, down_ref, y):
    field = []
    for i, (cx, cy, cz) in enumerate(VELOCITY):
        if 0 <= y - cy < NY:
            v = post_ref[PLACE[i], 1 - cx : 1 - cx + NX, y - cy, :]
        elif cy == 1:
            v = up_ref[Y_UP.index(i), HALO0 - cx : HALO0 - cx + NX, :]
        else:
            v = down_ref[Y_DOWN.index(i), HALO0 - cx : HALO0 - cx + NX, :]
        if cz == 1:
            v = pltpu.roll(v, 1, axis=1)
        elif cz == -1:
            v = pltpu.roll(v, NZ - 1, axis=1)
        field.append(v)
    return field


def split(x):
    hi = x.astype(BF16)
    lo = (x - hi.astype(F32)).astype(BF16)
    return hi, lo


def tall(rows, c, wide):
    return jnp.concatenate(
        [rows[pl.ds(c * wide + w, COLS, stride=PITCH), :] for w in range(wide)], axis=1
    )


def dot(a, b, ca, cb, precision=None):
    return lax.dot_general(
        a, b, (((ca,), (cb,)), ((), ())), precision=precision, preferred_element_type=F32
    )


def split3(x):
    hi = x.astype(BF16).astype(F32)
    mid = (x - hi).astype(BF16).astype(F32)
    return hi, mid, x - hi - mid


def outer8(r, t):
    h, m, l = split3(jnp.concatenate([r, t], axis=1))
    rh, rm, rl = h[:, 0:ZC], m[:, 0:ZC], l[:, 0:ZC]
    a = jnp.concatenate([rh, rh, rh, rm, rm, rl], axis=0).astype(BF16)
    b = jnp.concatenate([h, m, l, h, m, h], axis=0).astype(BF16)
    return dot(a, b, 0, 0)


def eliminate(rows, extra, first):
    d = [
        [jnp.broadcast_to(rows[i][:, first + j : first + j + 1], (1, ZC)) for j in range(i + 1)]
        for i in range(8)
    ]
    r, t = list(rows), list(extra)
    for j in range(8):
        inv = lax.rsqrt(d[j][j])
        r[j] = r[j] * inv
        t[j] = t[j] * inv
        col = [None if i <= j else d[i][j] * inv for i in range(8)]
        for i in range(j + 1, 8):
            for k in range(j + 1, i + 1):
                d[i][k] = d[i][k] - col[i] * col[k]
            r[i] = r[i] - col[i] * r[j]
            t[i] = t[i] - col[i] * t[j]
    return jnp.concatenate(r, axis=0), jnp.concatenate(t, axis=0)


def factor_block(b, work, inverse, upper):
    row8 = lax.broadcasted_iota(jnp.int32, (8, ZC), 0)
    lane8 = lax.broadcasted_iota(jnp.int32, (8, ZC), 1)
    o = 8 * b
    r, t = eliminate(
        [work[o + i : o + i + 1, :] for i in range(8)],
        [inverse[o + i : o + i + 1, :] for i in range(8)],
        o,
    )
    r = jnp.where(lane8 >= row8 + o, r, 0.0)
    upper[o : o + 8, :] = r
    inverse[o : o + 8, :] = t
    if o + 8 < COLS:
        change = outer8(r, t)
        work[o + 8 : COLS, :] = work[o + 8 : COLS, :] - change[o + 8 : COLS, 0:ZC]
        inverse[o + 8 : COLS, :] = inverse[o + 8 : COLS, :] - change[o + 8 : COLS, ZC:]


def main_kernel(
    nx,
    ny,
    pops_hbm,
    rate_hbm,
    mask_hbm,
    sv_hbm,
    basis_hbm,
    snaps_hbm,
    field_out,
    stack,
    inverse_ref,
    upper_ref,
    border_ref,
    pops,
    rate,
    mask,
    post_a,
    post_b,
    out_up,
    out_down,
    in_up,
    in_down,
    vel,
    pooled,
    gram,
    parts,
    recv_a,
    send_b,
    recv_b,
    recv_c,
    sums8,
    vec_b,
    vec_in_a,
    vec_in_b,
    sv,
    scale,
    work,
    plane_sem,
    load_sem,
    halo_send,
    halo_recv,
    red_send,
    red_recv,
):
    mx, my = lax.axis_index("gx"), lax.axis_index("gy")
    owners = COLS // 8
    posts = (post_a, post_b)

    def shifted(dx, dy):
        return (lax.rem(mx + (dx + nx), nx), lax.rem(my + (dy + ny), ny))

    def load_planes(g):
        part = pl.ds(4 * g, 4)
        return pltpu.make_async_copy(pops_hbm.at[:, part], pops.at[:, part], plane_sem.at[g])

    loads = [
        pltpu.make_async_copy(rate_hbm, rate, load_sem.at[0]),
        pltpu.make_async_copy(mask_hbm, mask, load_sem.at[1]),
        pltpu.make_async_copy(basis_hbm, stack.at[pl.ds(0, RANK), pl.ds(0, ROWS)], load_sem.at[2]),
        pltpu.make_async_copy(snaps_hbm, stack.at[pl.ds(RANK, OLD), pl.ds(0, ROWS)], load_sem.at[3]),
        pltpu.make_async_copy(sv_hbm, sv, load_sem.at[4]),
    ]
    for g in range(NX // 4):
        load_planes(g).start()
    loads[0].start()
    loads[1].start()

    barrier = pltpu.get_barrier_semaphore()

    def greet(to):
        pl.semaphore_signal(barrier, inc=1, device_id=to, device_id_type=MESH)

    for dx in (-1, 1):
        for dy in (-1, 1):
            greet(shifted(dx, dy))

    @pl.loop(0, nx - 1)
    def _(j):
        greet((lax.rem(mx + nx // 2 + j + lax.div(j, nx // 2), nx), my))

    @pl.loop(0, ny - 1)
    def _(j):
        greet((mx, lax.rem(my + ny // 2 + j + lax.div(j, ny // 2), ny)))

    loads[2].start()
    loads[3].start()
    loads[4].start()

    stack[COLS - 1] = jnp.zeros((PITCH, ZC), F32)
    scale[...] = jnp.ones_like(scale)

    def put(post, step, x):
        for i in range(19):
            posts[step][PLACE[i], x + 1] = post[i]

    def put_rows(post, step, x):
        for p, i in enumerate(Y_UP):
            out_up[step, p, pl.ds(x, 1), :] = post[i][NY - 1 : NY, :]
        for p, i in enumerate(Y_DOWN):
            out_down[step, p, pl.ds(x, 1), :] = post[i][0:1, :]

    def halo(step):
        post = posts[step]
        moves = []
        for i, plane, dx, dy in CORNERS:
            from_row = pl.ds(plane - 1, 1)
            at = pl.ds(HALO0 - 1 if dx == 1 else HALO0 + NX, 1)
            if dy == 1:
                p = Y_UP.index(i)
                moves.append((out_up.at[step, p, from_row, :], in_up.at[step, p, at, :], (dx, dy)))
            else:
                p = Y_DOWN.index(i)
                moves.append(
                    (out_down.at[step, p, from_row, :], in_down.at[step, p, at, :], (dx, dy))
                )
        inner = pl.ds(HALO0, NX)
        moves.append((out_up.at[step], in_up.at[step, :, inner, :], (0, 1)))
        moves.append((out_down.at[step], in_down.at[step, :, inner, :], (0, -1)))
        moves.append((post.at[pl.ds(0, 5), NX], post.at[pl.ds(0, 5), 0], (1, 0)))
        moves.append((post.at[pl.ds(5, 5), 1], post.at[pl.ds(5, 5), NX + 1], (-1, 0)))
        return [
            pltpu.make_async_remote_copy(
                src_ref=src,
                dst_ref=dst,
                send_sem=halo_send.at[step, k],
                recv_sem=halo_recv.at[step, k],
                device_id=shifted(*to),
                device_id_type=MESH,
            )
            for k, (src, dst, to) in enumerate(moves)
        ]

    loads[0].wait()
    loads[1].wait()
    for g in range(NX // 4):
        load_planes(g).wait()

        @pl.loop(4 * g, 4 * g + 4)
        def _(x):
            field = [pops[i, x] for i in range(19)]
            post = collide(field, rate[x], mask[x] > 0)
            put(post, 0, x)
            put_rows(post, 0, x)

    pl.semaphore_wait(barrier, (nx - 1) + (ny - 1) + 4)
    first = halo(0)
    for copy in first:
        copy.start()

    loads[2].wait()
    loads[3].wait()
    loads[4].wait()
    rows = stack.reshape(COLS * PITCH, ZC)
    gram[...] = jnp.zeros_like(gram)

    @pl.loop(0, ROWS // 32)
    def _(c):
        hi, lo = split(tall(rows, c, 32))
        gram[:, 0:COLS] += dot(jnp.concatenate([hi, lo], axis=0), hi, 1, 1)

    low = jnp.concatenate([gram[COLS : 2 * COLS, :], jnp.zeros((ZC - COLS, ZC), F32)], axis=0)
    parts[...] = gram[0:COLS, :] + low[0:COLS] + jnp.transpose(low)[0:COLS]

    def to_owner(j):
        peer = lax.rem(mx + j, nx)
        chunk = lax.rem(peer, owners)
        return peer, pltpu.make_async_remote_copy(
            src_ref=parts.at[pl.ds(pl.multiple_of(chunk * 8, 8), 8)],
            dst_ref=recv_a.at[mx],
            send_sem=red_send.at[0],
            recv_sem=red_recv.at[0],
            device_id=(peer, my),
            device_id_type=MESH,
        )

    @pl.loop(1, nx)
    def _(j):
        peer, copy = to_owner(j)

        @pl.when(peer < owners)
        def _():
            copy.start()

    own = pl.ds(pl.multiple_of(lax.rem(mx, owners) * 8, 8), 8)
    recv_a[mx] = parts[own, :]

    for copy in first:
        copy.wait_recv()
    second = halo(1)
    for y, group, out in ((NY - 1, Y_UP, out_up), (0, Y_DOWN, out_down)):
        field = arrive_face(post_a, in_up.at[0], in_down.at[0], y)
        post = collide(field, rate[:, y, :], mask[:, y, :] > 0)
        for p, i in enumerate(group):
            out[1, p] = post[i]
    for copy in second[0:6]:
        copy.start()

    @pl.loop(0, NX)
    def _(k):
        x = lax.rem(k + (NX - 1), NX)
        field = arrive(post_a, in_up.at[0], in_down.at[0], x)
        put(collide(field, rate[x], mask[x] > 0), 1, x)

        @pl.when(k == 1)
        def _():
            for copy in second[6:8]:
                copy.start()

    def all_along(src, dst, k, axis):
        def copy(j):
            if axis == 0:
                peer = (lax.rem(mx + j, nx), my)
            else:
                peer = (mx, lax.rem(my + j, ny))
            return pltpu.make_async_remote_copy(
                src_ref=src,
                dst_ref=dst,
                send_sem=red_send.at[k],
                recv_sem=red_recv.at[k],
                device_id=peer,
                device_id_type=MESH,
            )

        return copy

    def start_all(copy, count):
        @pl.loop(1, count)
        def _(j):
            copy(j).start()

    def wait_for(ref, sem):
        pltpu.make_async_copy(ref, ref, sem).wait()

    def total(ref, count):
        value = ref[0]
        for j in range(1, count):
            value = value + ref[j]
        return value

    ring_b = all_along(send_b.at[0], recv_b.at[my], 1, 1)
    ring_c = all_along(send_b.at[1], recv_c.at[mx], 2, 0)

    @pl.when(mx < owners)
    def _():
        wait_for(recv_a.at[pl.ds(0, nx - 1)], red_recv.at[0])
        value = total(recv_a, nx)
        send_b[0] = value
        recv_b[my] = value
        start_all(ring_b, ny)

    for copy in second:
        copy.wait_recv()


    @pl.loop(0, XC)
    def _(xc):
        sums = [None] * 3
        for half in range(2):
            x = 2 * xc + half
            field = arrive(post_b, in_up.at[1], in_down.at[1], x)
            for i in range(19):
                field_out[i, x] = field[i]
            fluid = mask[x] == 0
            for a, u in enumerate(flow(field)[1]):
                u = jnp.where(fluid, u, 0.0)
                sums[a] = u if half == 0 else sums[a] + u
        for a in range(3):
            vel[pl.ds(pl.multiple_of(a * XC * NY + xc * NY, NY), NY), :] = sums[a]

    @pl.when(mx < owners)
    def _():
        wait_for(recv_b.at[pl.ds(0, ny - 1)], red_recv.at[1])
        value = total(recv_b, ny)
        send_b[1] = value
        recv_c[mx] = value
        start_all(ring_c, nx)

    fine = lax.broadcasted_iota(jnp.int32, (NZ, ZC), 0)
    pair = lax.broadcasted_iota(jnp.int32, (NZ, ZC), 1)
    pick = jnp.where(fine // 2 == pair, SPEED_SCALE / 8.0, 0.0).astype(F32)
    pooled[...] = dot(vel[...], pick, 1, 0, HIGHEST)
    coarse = pooled[pl.ds(0, ROWS, stride=2), :] + pooled[pl.ds(1, ROWS, stride=2), :]
    stack[COLS - 1, 0:ROWS, :] = coarse

    tiles = ROWS // 8
    parted = coarse.reshape(tiles, 8, ZC)

    @pl.loop(0, COLS // 8)
    def _(k):
        for q in range(8):
            column = stack[k * 8 + q, 0:ROWS, :].reshape(tiles, 8, ZC)
            sums8[pl.ds(pl.multiple_of(k * 64 + q * 8, 8), 8), :] = jnp.sum(column * parted, axis=0)

    folded = sums8[pl.ds(0, COLS, stride=8), :]
    for q in range(1, 8):
        folded = folded + sums8[pl.ds(q, COLS, stride=8), :]
    folded = jnp.concatenate([folded, jnp.zeros((ZC - COLS, ZC), F32)], axis=0)
    last = dot(jnp.ones((8, ZC), F32), folded, 1, 1, HIGHEST)
    one = pl.ds(0, 1)
    vec_b[0] = last
    vec_in_a[mx] = last
    ring_d = all_along(vec_b.at[0, one], vec_in_a.at[mx, one], 3, 0)
    start_all(ring_d, nx)

    def vec_total(ref, count):
        value = ref[0, 0:1, :]
        for j in range(1, count):
            value = value + ref[j, 0:1, :]
        return value

    wait_for(vec_in_a.at[pl.ds(0, nx - 1), one], red_recv.at[3])
    value = jnp.broadcast_to(vec_total(vec_in_a, nx), (8, ZC))
    vec_b[1] = value
    vec_in_b[my] = value
    ring_e = all_along(vec_b.at[1, one], vec_in_b.at[my, one], 4, 1)
    start_all(ring_e, ny)

    @pl.when(mx < owners)
    def _():
        wait_for(recv_c.at[pl.ds(0, owners - 1)], red_recv.at[2])

    @pl.when(mx >= owners)
    def _():
        wait_for(recv_c.at[pl.ds(0, owners)], red_recv.at[2])

    row = lax.broadcasted_iota(jnp.int32, (COLS, ZC), 0)
    lane = lax.broadcasted_iota(jnp.int32, (COLS, ZC), 1)
    scale[0:1, 0:RANK] = sv[...]
    srow = scale[0:1, :]
    scol = jnp.sum(jnp.where(row == lane, srow, 0.0), axis=1, keepdims=True)
    per_row = 1.0 / (all_rows(nx, ny))
    whole = jnp.concatenate([recv_c[c] for c in range(owners)], axis=0)
    whole = whole * (srow * scol) * per_row
    whole = jnp.where((row == COLS - 1) & (lane == COLS - 1), 1.0, whole)

    work[...] = whole
    inverse_ref[...] = (row == lane).astype(F32)

    half = 0
    for b in range(half):
        factor_block(b, work, inverse_ref, upper_ref)

    for b in range(half, owners):
        factor_block(b, work, inverse_ref, upper_ref)

    wait_for(vec_in_b.at[pl.ds(0, ny - 1), one], red_recv.at[4])
    border_ref[0:4, :] = jnp.broadcast_to(vec_total(vec_in_b, ny) * srow * per_row, (4, ZC))
    border_ref[4:8, :] = jnp.broadcast_to(srow, (4, ZC))

    for copy in first + second:
        copy.wait_send()

    @pl.when(mx < owners)
    def _():
        wait_for(recv_a.at[pl.ds(0, owners - 1)], red_send.at[0])
        wait_for(recv_b.at[pl.ds(0, ny - 1)], red_send.at[1])
        wait_for(recv_a.at[pl.ds(0, nx - 1)], red_send.at[2])

    @pl.when(mx >= owners)
    def _():
        wait_for(recv_a.at[pl.ds(0, owners)], red_send.at[0])

    wait_for(vec_in_a.at[pl.ds(0, nx - 1), one], red_send.at[3])
    wait_for(vec_in_b.at[pl.ds(0, ny - 1), one], red_send.at[4])


def all_rows(nx, ny):
    return float(ROWS * ZC * nx * ny)


def finish_kernel(
    field_ref,
    stack,
    inverse_ref,
    upper_ref,
    border_ref,
    pops_hbm,
    factor_ref,
    new_hbm,
    fresh,
    left,
    sem,
):
    wide = 16
    field = pltpu.make_async_copy(field_ref, pops_hbm, sem.at[ROWS // wide])
    field.start()

    row = lax.broadcasted_iota(jnp.int32, (COLS, ZC), 0)
    lane = lax.broadcasted_iota(jnp.int32, (COLS, ZC), 1)
    inverse = inverse_ref[...]
    border = border_ref[0:1, :]
    scale = border_ref[4:5, :]
    old = jnp.where(lane[0:1] < COLS - 1, border, 0.0)
    lcol = dot(inverse, jnp.broadcast_to(old, (ZC, ZC)), 1, 1, HIGHEST)
    lcol = jnp.where(row < COLS - 1, lcol, 0.0)
    square = border[0:1, COLS - 1 : COLS] - jnp.sum(lcol * lcol, axis=0, keepdims=True)
    inv = lax.rsqrt(square)
    end = jnp.where(row == COLS - 1, square * inv, lcol)
    factor_ref[...] = jnp.where(lane == COLS - 1, end, upper_ref[...])[:, 0:COLS]
    bottom = jnp.sum(lcol * inverse, axis=0, keepdims=True)
    bottom = jnp.where(lane[0:1] == COLS - 1, inv, -bottom * inv)
    inverse = jnp.where(row == COLS - 1, bottom, inverse) * scale

    hi = inverse.astype(BF16).astype(F32)
    lo = inverse - hi
    none = jnp.zeros_like(hi)
    hi, lo = jnp.concatenate([hi, none], axis=1), jnp.concatenate([lo, none], axis=1)
    placed = hi + pltpu.roll(lo, COLS, axis=1) + pltpu.roll(hi, 2 * COLS, axis=1)
    left[...] = placed.astype(BF16)

    rows = stack.reshape(COLS * PITCH, ZC)
    made = fresh.reshape(COLS * PITCH, ZC)

    def store(c):
        part = pl.ds(pl.multiple_of(c * wide, wide), wide)
        return pltpu.make_async_copy(fresh.at[:, part], new_hbm.at[:, part], sem.at[c])

    @pl.loop(0, ROWS // wide)
    def _(c):
        hi, lo = split(tall(rows, c, wide))
        result = dot(left[:, 0 : 3 * COLS], jnp.concatenate([hi, hi, lo], axis=0), 1, 0)
        for w in range(wide):
            made[pl.ds(c * wide + w, COLS, stride=PITCH), :] = result[:, w * ZC : (w + 1) * ZC]
        store(c).start()

    @pl.loop(0, ROWS // wide)
    def _(c):
        store(c).wait()

    field.wait()


def on_device(nx, ny, pops, rate, mask, sv, basis, snaps):
    sv = sv.reshape(1, RANK)
    basis = basis.reshape(RANK, ROWS, ZC)
    snaps = snaps.reshape(OLD, ROWS, ZC)
    given = (pops, rate, mask, sv, basis, snaps)
    given = [pltpu.with_memory_space_constraint(x, pltpu.HBM) for x in given]
    far = pl.BlockSpec(memory_space=pltpu.HBM)
    here = pl.BlockSpec(memory_space=pltpu.VMEM)
    owners = COLS // 8

    def f32(*shape):
        return jax.ShapeDtypeStruct(shape, F32)

    def vmem(*shape):
        return pltpu.VMEM(shape, F32)

    dma = pltpu.SemaphoreType.DMA
    field, stack, inverse, upper, border = pl.pallas_call(
        functools.partial(main_kernel, nx, ny),
        out_shape=(
            f32(19, NX, NY, NZ),
            f32(COLS, PITCH, ZC),
            f32(COLS, ZC),
            f32(COLS, ZC),
            f32(8, ZC),
        ),
        in_specs=[far] * 6,
        out_specs=(here,) * 5,
        scratch_shapes=[
            vmem(19, NX, NY, NZ),
            vmem(NX, NY, NZ),
            pltpu.VMEM((NX, NY, NZ), jnp.int32),
            vmem(19, NX + 2, NY, NZ),
            vmem(19, NX + 2, NY, NZ),
            vmem(2, 5, NX, NZ),
            vmem(2, 5, NX, NZ),
            vmem(2, 5, NX + 16, NZ),
            vmem(2, 5, NX + 16, NZ),
            vmem(3 * XC * NY, NZ),
            vmem(3 * XC * NY, ZC),
            vmem(2 * COLS, ZC),
            vmem(COLS, ZC),
            vmem(nx, 8, ZC),
            vmem(2, 8, ZC),
            vmem(ny, 8, ZC),
            vmem(owners, 8, ZC),
            vmem(8 * COLS, ZC),
            vmem(2, 8, ZC),
            vmem(nx, 8, ZC),
            vmem(ny, 8, ZC),
            vmem(1, RANK),
            vmem(8, ZC),
            vmem(COLS, ZC),
            dma((NX // 4,)),
            dma((5,)),
            dma((2, 8)),
            dma((2, 8)),
            dma((5,)),
            dma((5,)),
        ],
        compiler_params=pltpu.CompilerParams(
            collective_id=0, has_side_effects=True, vmem_limit_bytes=40 * 2**20
        ),
        name="substeps",
    )(*given)
    out, factor, new = pl.pallas_call(
        finish_kernel,
        out_shape=(f32(19, NX, NY, NZ), f32(COLS, COLS), f32(COLS, ROWS, ZC)),
        in_specs=[here] * 5,
        out_specs=(far, here, far),
        scratch_shapes=[
            vmem(COLS, PITCH, ZC),
            pltpu.VMEM((COLS, 2 * ZC), BF16),
            dma((ROWS // 16 + 1,)),
        ],
        compiler_params=pltpu.CompilerParams(vmem_limit_bytes=24 * 2**20),
        name="finish",
    )(field, stack, inverse, upper, border)
    return out, factor, new.reshape(COLS, 3, XC, YC, ZC)


def solution(mesh):
    return jax.shard_map(
        functools.partial(on_device, mesh.shape["gx"], mesh.shape["gy"]),
        mesh=mesh,
        in_specs=(
            P(None, "gx", "gy", None),
            P("gx", "gy", None),
            P("gx", "gy", None),
            P(),
            P(None, None, "gx", "gy", None),
            P(None, None, "gx", "gy", None),
        ),
        out_specs=(P(None, "gx", "gy", None), P(), P(None, None, "gx", "gy", None)),
        check_vma=False,
    )
```

```python
import functools

import jax
import jax.numpy as jnp
from jax import lax
from jax.experimental import pallas as pl
from jax.experimental.pallas import tpu as pltpu
from jax.sharding import PartitionSpec as P

MESH = pl.DeviceIdType.MESH
HIGHEST = lax.Precision.HIGHEST
F32 = jnp.float32
BF16 = jnp.bfloat16

VELOCITY = [
    (0, 0, 0),
    (1, 0, 0),
    (-1, 0, 0),
    (0, 1, 0),
    (0, -1, 0),
    (0, 0, 1),
    (0, 0, -1),
    (1, 1, 0),
    (-1, -1, 0),
    (1, -1, 0),
    (-1, 1, 0),
    (1, 0, 1),
    (-1, 0, -1),
    (1, 0, -1),
    (-1, 0, 1),
    (0, 1, 1),
    (0, -1, -1),
    (0, 1, -1),
    (0, -1, 1),
]
SPEED_SCALE = 10.0

ORDER = [1, 7, 9, 11, 13, 2, 8, 10, 12, 14, 0, 3, 4, 5, 6, 15, 16, 17, 18]
PLACE = [ORDER.index(i) for i in range(19)]
Y_UP = [3, 7, 10, 15, 17]
Y_DOWN = [4, 8, 9, 16, 18]
CORNERS = [(7, 16, 1, 1), (8, 1, -1, -1), (9, 16, 1, -1), (10, 1, -1, 1)]

NX, NY, NZ = 16, 8, 256
XC, YC, ZC = 8, 4, 128
COLS, RANK, OLD = 80, 64, 15
ROWS = 3 * XC * YC
PITCH = ROWS + 8
HALO0 = 8


def flow(field):
    plus = [field[i] + field[i + 1] for i in range(1, 19, 2)]
    diff = [field[i] - field[i + 1] for i in range(1, 19, 2)]
    rho = field[0]
    for s in plus:
        rho = rho + s
    comps = []
    for axis in range(3):
        total = None
        for p, d in enumerate(diff):
            c = VELOCITY[2 * p + 1][axis]
            if c:
                total = d if total is None else (total + d if c > 0 else total - d)
        comps.append(total)
    inv = 1.0 / rho
    return rho, [c * inv for c in comps]


def collide(field, rate, solid):
    rho, vel = flow(field)
    tri = [3.0 * u for u in vel]
    base = 1.0 - 1.5 * (vel[0] * vel[0] + vel[1] * vel[1] + vel[2] * vel[2])
    post = [None] * 19
    face = rho * (1.0 / 18.0)
    edge = rho * (1.0 / 36.0)
    rest = rho * (1.0 / 3.0) * base
    post[0] = jnp.where(solid, field[0], field[0] + rate * (rest - field[0]))
    for i in range(1, 19, 2):
        along = None
        for axis in range(3):
            c = VELOCITY[i][axis]
            if c:
                along = (
                    tri[axis]
                    if along is None
                    else (along + tri[axis] if c > 0 else along - tri[axis])
                )
        weight = face if i < 7 else edge
        even = weight * (base + 0.5 * (along * along))
        odd = weight * along
        fp, fm = field[i], field[i + 1]
        post[i] = jnp.where(solid, fm, fp + rate * ((even + odd) - fp))
        post[i + 1] = jnp.where(solid, fp, fm + rate * ((even - odd) - fm))
    return post


def arrive(post_ref, up_ref, down_ref, x):
    row = lax.broadcasted_iota(jnp.int32, (NY, NZ), 0)
    field = []
    for i, (cx, cy, cz) in enumerate(VELOCITY):
        v = post_ref[PLACE[i], x + 1 - cx]
        if cy == 1:
            halo = up_ref[Y_UP.index(i), pl.ds(x + HALO0 - cx, 1), :]
            v = jnp.where(row == 0, halo, pltpu.roll(v, 1, axis=0))
        elif cy == -1:
            halo = down_ref[Y_DOWN.index(i), pl.ds(x + HALO0 - cx, 1), :]
            v = jnp.where(row == NY - 1, halo, pltpu.roll(v, NY - 1, axis=0))
        if cz == 1:
            v = pltpu.roll(v, 1, axis=1)
        elif cz == -1:
            v = pltpu.roll(v, NZ - 1, axis=1)
        field.append(v)
    return field


def arrive_face(post_ref, up_ref, down_ref, y):
    field = []
    for i, (cx, cy, cz) in enumerate(VELOCITY):
        if 0 <= y - cy < NY:
            v = post_ref[PLACE[i], 1 - cx : 1 - cx + NX, y - cy, :]
        elif cy == 1:
            v = up_ref[Y_UP.index(i), HALO0 - cx : HALO0 - cx + NX, :]
        else:
            v = down_ref[Y_DOWN.index(i), HALO0 - cx : HALO0 - cx + NX, :]
        if cz == 1:
            v = pltpu.roll(v, 1, axis=1)
        elif cz == -1:
            v = pltpu.roll(v, NZ - 1, axis=1)
        field.append(v)
    return field


def split(x):
    hi = x.astype(BF16)
    lo = (x - hi.astype(F32)).astype(BF16)
    return hi, lo


def tall(rows, c, wide):
    return jnp.concatenate(
        [rows[pl.ds(c * wide + w, COLS, stride=PITCH), :] for w in range(wide)], axis=1
    )


def dot(a, b, ca, cb, precision=None):
    return lax.dot_general(
        a, b, (((ca,), (cb,)), ((), ())), precision=precision, preferred_element_type=F32
    )


def split3(x):
    hi = x.astype(BF16).astype(F32)
    mid = (x - hi).astype(BF16).astype(F32)
    return hi, mid, x - hi - mid


def outer8(r, t):
    h, m, l = split3(jnp.concatenate([r, t], axis=1))
    rh, rm, rl = h[:, 0:ZC], m[:, 0:ZC], l[:, 0:ZC]
    a = jnp.concatenate([rh, rh, rh, rm, rm, rl], axis=0).astype(BF16)
    b = jnp.concatenate([h, m, l, h, m, h], axis=0).astype(BF16)
    return dot(a, b, 0, 0)


def eliminate(rows, extra, first):
    d = [
        [jnp.broadcast_to(rows[i][:, first + j : first + j + 1], (1, ZC)) for j in range(i + 1)]
        for i in range(8)
    ]
    r, t = list(rows), list(extra)
    for j in range(8):
        inv = lax.rsqrt(d[j][j])
        r[j] = r[j] * inv
        t[j] = t[j] * inv
        col = [None if i <= j else d[i][j] * inv for i in range(8)]
        for i in range(j + 1, 8):
            for k in range(j + 1, i + 1):
                d[i][k] = d[i][k] - col[i] * col[k]
            r[i] = r[i] - col[i] * r[j]
            t[i] = t[i] - col[i] * t[j]
    return jnp.concatenate(r, axis=0), jnp.concatenate(t, axis=0)


def factor_block(b, work, inverse, upper):
    row8 = lax.broadcasted_iota(jnp.int32, (8, ZC), 0)
    lane8 = lax.broadcasted_iota(jnp.int32, (8, ZC), 1)
    o = 8 * b
    r, t = eliminate(
        [work[o + i : o + i + 1, :] for i in range(8)],
        [inverse[o + i : o + i + 1, :] for i in range(8)],
        o,
    )
    r = jnp.where(lane8 >= row8 + o, r, 0.0)
    upper[o : o + 8, :] = r
    inverse[o : o + 8, :] = t
    if o + 8 < COLS:
        change = outer8(r, t)
        work[o + 8 : COLS, :] = work[o + 8 : COLS, :] - change[o + 8 : COLS, 0:ZC]
        inverse[o + 8 : COLS, :] = inverse[o + 8 : COLS, :] - change[o + 8 : COLS, ZC:]


def main_kernel(
    nx,
    ny,
    pops_hbm,
    rate_hbm,
    mask_hbm,
    sv_hbm,
    basis_hbm,
    snaps_hbm,
    field_out,
    stack,
    inverse_ref,
    upper_ref,
    border_ref,
    left,
    pops,
    rate,
    mask,
    post_a,
    post_b,
    out_up,
    out_down,
    in_up,
    in_down,
    vel,
    pooled,
    gram,
    parts,
    recv_a,
    send_b,
    recv_b,
    recv_c,
    sums8,
    vec_b,
    vec_in_a,
    vec_in_b,
    sv,
    scale,
    work,
    plane_sem,
    load_sem,
    halo_send,
    halo_recv,
    red_send,
    red_recv,
):
    mx, my = lax.axis_index("gx"), lax.axis_index("gy")
    owners = COLS // 8
    posts = (post_a, post_b)

    def shifted(dx, dy):
        return (lax.rem(mx + (dx + nx), nx), lax.rem(my + (dy + ny), ny))

    def load_planes(g):
        part = pl.ds(4 * g, 4)
        return pltpu.make_async_copy(pops_hbm.at[:, part], pops.at[:, part], plane_sem.at[g])

    loads = [
        pltpu.make_async_copy(rate_hbm, rate, load_sem.at[0]),
        pltpu.make_async_copy(mask_hbm, mask, load_sem.at[1]),
        pltpu.make_async_copy(basis_hbm, stack.at[pl.ds(0, RANK), pl.ds(0, ROWS)], load_sem.at[2]),
        pltpu.make_async_copy(snaps_hbm, stack.at[pl.ds(RANK, OLD), pl.ds(0, ROWS)], load_sem.at[3]),
        pltpu.make_async_copy(sv_hbm, sv, load_sem.at[4]),
    ]
    for g in range(NX // 4):
        load_planes(g).start()
    loads[0].start()
    loads[1].start()

    barrier = pltpu.get_barrier_semaphore()

    def greet(to):
        pl.semaphore_signal(barrier, inc=1, device_id=to, device_id_type=MESH)

    for dx in (-1, 1):
        for dy in (-1, 1):
            greet(shifted(dx, dy))

    @pl.loop(0, nx - 1)
    def _(j):
        greet((lax.rem(mx + nx // 2 + j + lax.div(j, nx // 2), nx), my))

    @pl.loop(0, ny - 1)
    def _(j):
        greet((mx, lax.rem(my + ny // 2 + j + lax.div(j, ny // 2), ny)))

    loads[2].start()
    loads[3].start()
    loads[4].start()

    stack[COLS - 1] = jnp.zeros((PITCH, ZC), F32)
    scale[...] = jnp.ones_like(scale)

    def put(post, step, x):
        for i in range(19):
            posts[step][PLACE[i], x + 1] = post[i]

    def put_rows(post, step, x):
        for p, i in enumerate(Y_UP):
            out_up[step, p, pl.ds(x, 1), :] = post[i][NY - 1 : NY, :]
        for p, i in enumerate(Y_DOWN):
            out_down[step, p, pl.ds(x, 1), :] = post[i][0:1, :]

    def halo(step):
        post = posts[step]
        moves = []
        for i, plane, dx, dy in CORNERS:
            from_row = pl.ds(plane - 1, 1)
            at = pl.ds(HALO0 - 1 if dx == 1 else HALO0 + NX, 1)
            if dy == 1:
                p = Y_UP.index(i)
                moves.append((out_up.at[step, p, from_row, :], in_up.at[step, p, at, :], (dx, dy)))
            else:
                p = Y_DOWN.index(i)
                moves.append(
                    (out_down.at[step, p, from_row, :], in_down.at[step, p, at, :], (dx, dy))
                )
        inner = pl.ds(HALO0, NX)
        moves.append((out_up.at[step], in_up.at[step, :, inner, :], (0, 1)))
        moves.append((out_down.at[step], in_down.at[step, :, inner, :], (0, -1)))
        moves.append((post.at[pl.ds(0, 5), NX], post.at[pl.ds(0, 5), 0], (1, 0)))
        moves.append((post.at[pl.ds(5, 5), 1], post.at[pl.ds(5, 5), NX + 1], (-1, 0)))
        return [
            pltpu.make_async_remote_copy(
                src_ref=src,
                dst_ref=dst,
                send_sem=halo_send.at[step, k],
                recv_sem=halo_recv.at[step, k],
                device_id=shifted(*to),
                device_id_type=MESH,
            )
            for k, (src, dst, to) in enumerate(moves)
        ]

    loads[0].wait()
    loads[1].wait()
    for g in range(NX // 4):
        load_planes(g).wait()

        @pl.loop(4 * g, 4 * g + 4)
        def _(x):
            field = [pops[i, x] for i in range(19)]
            post = collide(field, rate[x], mask[x] > 0)
            put(post, 0, x)
            put_rows(post, 0, x)

    pl.semaphore_wait(barrier, (nx - 1) + (ny - 1) + 4)
    first = halo(0)
    for copy in first:
        copy.start()

    loads[2].wait()
    loads[3].wait()
    loads[4].wait()
    rows = stack.reshape(COLS * PITCH, ZC)
    gram[...] = jnp.zeros_like(gram)

    @pl.loop(0, ROWS // 32)
    def _(c):
        hi, lo = split(tall(rows, c, 32))
        gram[:, 0:COLS] += dot(jnp.concatenate([hi, lo], axis=0), hi, 1, 1)

    low = jnp.concatenate([gram[COLS : 2 * COLS, :], jnp.zeros((ZC - COLS, ZC), F32)], axis=0)
    parts[...] = gram[0:COLS, :] + low[0:COLS] + jnp.transpose(low)[0:COLS]

    def to_owner(j):
        peer = lax.rem(mx + j, nx)
        chunk = lax.rem(peer, owners)
        return peer, pltpu.make_async_remote_copy(
            src_ref=parts.at[pl.ds(pl.multiple_of(chunk * 8, 8), 8)],
            dst_ref=recv_a.at[mx],
            send_sem=red_send.at[0],
            recv_sem=red_recv.at[0],
            device_id=(peer, my),
            device_id_type=MESH,
        )

    @pl.loop(1, nx)
    def _(j):
        peer, copy = to_owner(j)

        @pl.when(peer < owners)
        def _():
            copy.start()

    own = pl.ds(pl.multiple_of(lax.rem(mx, owners) * 8, 8), 8)
    recv_a[mx] = parts[own, :]

    for copy in first:
        copy.wait_recv()
    second = halo(1)
    for y, group, out in ((NY - 1, Y_UP, out_up), (0, Y_DOWN, out_down)):
        field = arrive_face(post_a, in_up.at[0], in_down.at[0], y)
        post = collide(field, rate[:, y, :], mask[:, y, :] > 0)
        for p, i in enumerate(group):
            out[1, p] = post[i]
    for copy in second[0:6]:
        copy.start()

    @pl.loop(0, NX)
    def _(k):
        x = lax.rem(k + (NX - 1), NX)
        field = arrive(post_a, in_up.at[0], in_down.at[0], x)
        put(collide(field, rate[x], mask[x] > 0), 1, x)

        @pl.when(k == 1)
        def _():
            for copy in second[6:8]:
                copy.start()

    def all_along(src, dst, k, axis):
        def copy(j):
            if axis == 0:
                peer = (lax.rem(mx + j, nx), my)
            else:
                peer = (mx, lax.rem(my + j, ny))
            return pltpu.make_async_remote_copy(
                src_ref=src,
                dst_ref=dst,
                send_sem=red_send.at[k],
                recv_sem=red_recv.at[k],
                device_id=peer,
                device_id_type=MESH,
            )

        return copy

    def start_all(copy, count):
        @pl.loop(1, count)
        def _(j):
            copy(j).start()

    def wait_for(ref, sem):
        pltpu.make_async_copy(ref, ref, sem).wait()

    def total(ref, count):
        value = ref[0]
        for j in range(1, count):
            value = value + ref[j]
        return value

    ring_b = all_along(send_b.at[0], recv_b.at[my], 1, 1)
    ring_c = all_along(send_b.at[1], recv_c.at[mx], 2, 0)

    @pl.when(mx < owners)
    def _():
        wait_for(recv_a.at[pl.ds(0, nx - 1)], red_recv.at[0])
        value = total(recv_a, nx)
        send_b[0] = value
        recv_b[my] = value
        start_all(ring_b, ny)

    for copy in second:
        copy.wait_recv()


    @pl.loop(0, XC)
    def _(xc):
        sums = [None] * 3
        for half in range(2):
            x = 2 * xc + half
            field = arrive(post_b, in_up.at[1], in_down.at[1], x)
            for i in range(19):
                field_out[i, x] = field[i]
            fluid = mask[x] == 0
            for a, u in enumerate(flow(field)[1]):
                u = jnp.where(fluid, u, 0.0)
                sums[a] = u if half == 0 else sums[a] + u
        for a in range(3):
            vel[pl.ds(pl.multiple_of(a * XC * NY + xc * NY, NY), NY), :] = sums[a]

    @pl.when(mx < owners)
    def _():
        wait_for(recv_b.at[pl.ds(0, ny - 1)], red_recv.at[1])
        value = total(recv_b, ny)
        send_b[1] = value
        recv_c[mx] = value
        start_all(ring_c, nx)

    fine = lax.broadcasted_iota(jnp.int32, (NZ, ZC), 0)
    pair = lax.broadcasted_iota(jnp.int32, (NZ, ZC), 1)
    pick = jnp.where(fine // 2 == pair, SPEED_SCALE / 8.0, 0.0).astype(F32)
    pooled[...] = dot(vel[...], pick, 1, 0, HIGHEST)
    coarse = pooled[pl.ds(0, ROWS, stride=2), :] + pooled[pl.ds(1, ROWS, stride=2), :]
    stack[COLS - 1, 0:ROWS, :] = coarse

    tiles = ROWS // 8
    parted = coarse.reshape(tiles, 8, ZC)

    @pl.loop(0, COLS // 8)
    def _(k):
        for q in range(8):
            column = stack[k * 8 + q, 0:ROWS, :].reshape(tiles, 8, ZC)
            sums8[pl.ds(pl.multiple_of(k * 64 + q * 8, 8), 8), :] = jnp.sum(column * parted, axis=0)

    folded = sums8[pl.ds(0, COLS, stride=8), :]
    for q in range(1, 8):
        folded = folded + sums8[pl.ds(q, COLS, stride=8), :]
    folded = jnp.concatenate([folded, jnp.zeros((ZC - COLS, ZC), F32)], axis=0)
    last = dot(jnp.ones((8, ZC), F32), folded, 1, 1, HIGHEST)
    one = pl.ds(0, 1)
    vec_b[0] = last
    vec_in_a[mx] = last
    ring_d = all_along(vec_b.at[0, one], vec_in_a.at[mx, one], 3, 0)
    start_all(ring_d, nx)

    def vec_total(ref, count):
        value = ref[0, 0:1, :]
        for j in range(1, count):
            value = value + ref[j, 0:1, :]
        return value

    wait_for(vec_in_a.at[pl.ds(0, nx - 1), one], red_recv.at[3])
    value = jnp.broadcast_to(vec_total(vec_in_a, nx), (8, ZC))
    vec_b[1] = value
    vec_in_b[my] = value
    ring_e = all_along(vec_b.at[1, one], vec_in_b.at[my, one], 4, 1)
    start_all(ring_e, ny)

    @pl.when(mx < owners)
    def _():
        wait_for(recv_c.at[pl.ds(0, owners - 1)], red_recv.at[2])

    @pl.when(mx >= owners)
    def _():
        wait_for(recv_c.at[pl.ds(0, owners)], red_recv.at[2])

    row = lax.broadcasted_iota(jnp.int32, (COLS, ZC), 0)
    lane = lax.broadcasted_iota(jnp.int32, (COLS, ZC), 1)
    scale[0:1, 0:RANK] = sv[...]
    srow = scale[0:1, :]
    scol = jnp.sum(jnp.where(row == lane, srow, 0.0), axis=1, keepdims=True)
    per_row = 1.0 / (all_rows(nx, ny))
    whole = jnp.concatenate([recv_c[c] for c in range(owners)], axis=0)
    whole = whole * (srow * scol) * per_row
    whole = jnp.where((row == COLS - 1) & (lane == COLS - 1), 1.0, whole)

    work[...] = whole
    inverse_ref[...] = (row == lane).astype(F32)

    half = 0
    for b in range(half):
        factor_block(b, work, inverse_ref, upper_ref)

    for b in range(half, owners):
        factor_block(b, work, inverse_ref, upper_ref)

    inverse = inverse_ref[...] * srow
    hi = inverse.astype(BF16).astype(F32)
    lo = inverse - hi
    none = jnp.zeros_like(hi)
    hi, lo = jnp.concatenate([hi, none], axis=1), jnp.concatenate([lo, none], axis=1)
    placed = hi + pltpu.roll(lo, COLS, axis=1) + pltpu.roll(hi, 2 * COLS, axis=1)
    left[...] = placed.astype(BF16)

    wait_for(vec_in_b.at[pl.ds(0, ny - 1), one], red_recv.at[4])
    border_ref[...] = jnp.broadcast_to(vec_total(vec_in_b, ny) * srow * per_row, (8, ZC))

    for copy in first + second:
        copy.wait_send()

    @pl.when(mx < owners)
    def _():
        wait_for(recv_a.at[pl.ds(0, owners - 1)], red_send.at[0])
        wait_for(recv_b.at[pl.ds(0, ny - 1)], red_send.at[1])
        wait_for(recv_a.at[pl.ds(0, nx - 1)], red_send.at[2])

    @pl.when(mx >= owners)
    def _():
        wait_for(recv_a.at[pl.ds(0, owners)], red_send.at[0])

    wait_for(vec_in_a.at[pl.ds(0, nx - 1), one], red_send.at[3])
    wait_for(vec_in_b.at[pl.ds(0, ny - 1), one], red_send.at[4])


def all_rows(nx, ny):
    return float(ROWS * ZC * nx * ny)


def finish_kernel(
    field_ref,
    stack,
    inverse_ref,
    upper_ref,
    border_ref,
    left,
    pops_hbm,
    factor_ref,
    new_hbm,
    fresh,
    column,
    newest,
    sem,
):
    wide = 32
    field = pltpu.make_async_copy(field_ref, pops_hbm, sem.at[ROWS // wide])
    field.start()

    rows = stack.reshape(COLS * PITCH, ZC)
    made = fresh.reshape(COLS * PITCH, ZC)

    done = pl.ds(0, COLS - 1)

    def store(c):
        part = pl.ds(pl.multiple_of(c * wide, wide), wide)
        return pltpu.make_async_copy(fresh.at[done, part], new_hbm.at[done, part], sem.at[c])

    @pl.loop(0, ROWS // wide)
    def _(c):
        hi, lo = split(tall(rows, c, wide))
        result = dot(left[:, 0 : 3 * COLS], jnp.concatenate([hi, hi, lo], axis=0), 1, 0)
        for w in range(wide):
            made[pl.ds(c * wide + w, COLS, stride=PITCH), :] = result[:, w * ZC : (w + 1) * ZC]
        store(c).start()

    row = lax.broadcasted_iota(jnp.int32, (COLS, ZC), 0)
    lane = lax.broadcasted_iota(jnp.int32, (COLS, ZC), 1)
    inverse = inverse_ref[...]
    border = border_ref[0:1, :]
    old = jnp.where(lane[0:1] < COLS - 1, border, 0.0)
    lcol = dot(inverse, jnp.broadcast_to(old, (ZC, ZC)), 1, 1, HIGHEST)
    lcol = jnp.where(row < COLS - 1, lcol, 0.0)
    column[...] = lcol
    square = border[0:1, COLS - 1 : COLS] - jnp.sum(lcol * lcol, axis=0, keepdims=True)
    inv = lax.rsqrt(square)
    end = jnp.where(row == COLS - 1, square * inv, lcol)
    factor_ref[...] = jnp.where(lane == COLS - 1, end, upper_ref[...])[:, 0:COLS]

    def minus(k, value):
        for q in range(8):
            i = k * 8 + q
            value = value - column[pl.ds(i, 1), :] * fresh[i, 0:ROWS, :]
        return value

    value = stack[COLS - 1, 0:ROWS, :]
    newest[...] = lax.fori_loop(0, COLS // 8, minus, value) * inv
    last = pltpu.make_async_copy(newest, new_hbm.at[COLS - 1], sem.at[ROWS // wide + 1])
    last.start()
    last.wait()

    @pl.loop(0, ROWS // wide)
    def _(c):
        store(c).wait()

    field.wait()


def on_device(nx, ny, pops, rate, mask, sv, basis, snaps):
    sv = sv.reshape(1, RANK)
    basis = basis.reshape(RANK, ROWS, ZC)
    snaps = snaps.reshape(OLD, ROWS, ZC)
    given = (pops, rate, mask, sv, basis, snaps)
    given = [pltpu.with_memory_space_constraint(x, pltpu.HBM) for x in given]
    far = pl.BlockSpec(memory_space=pltpu.HBM)
    here = pl.BlockSpec(memory_space=pltpu.VMEM)
    owners = COLS // 8

    def f32(*shape):
        return jax.ShapeDtypeStruct(shape, F32)

    def vmem(*shape):
        return pltpu.VMEM(shape, F32)

    dma = pltpu.SemaphoreType.DMA
    field, stack, inverse, upper, border, left = pl.pallas_call(
        functools.partial(main_kernel, nx, ny),
        out_shape=(
            f32(19, NX, NY, NZ),
            f32(COLS, PITCH, ZC),
            f32(COLS, ZC),
            f32(COLS, ZC),
            f32(8, ZC),
            jax.ShapeDtypeStruct((COLS, 2 * ZC), BF16),
        ),
        in_specs=[far] * 6,
        out_specs=(here,) * 6,
        scratch_shapes=[
            vmem(19, NX, NY, NZ),
            vmem(NX, NY, NZ),
            pltpu.VMEM((NX, NY, NZ), jnp.int32),
            vmem(19, NX + 2, NY, NZ),
            vmem(19, NX + 2, NY, NZ),
            vmem(2, 5, NX, NZ),
            vmem(2, 5, NX, NZ),
            vmem(2, 5, NX + 16, NZ),
            vmem(2, 5, NX + 16, NZ),
            vmem(3 * XC * NY, NZ),
            vmem(3 * XC * NY, ZC),
            vmem(2 * COLS, ZC),
            vmem(COLS, ZC),
            vmem(nx, 8, ZC),
            vmem(2, 8, ZC),
            vmem(ny, 8, ZC),
            vmem(owners, 8, ZC),
            vmem(8 * COLS, ZC),
            vmem(2, 8, ZC),
            vmem(nx, 8, ZC),
            vmem(ny, 8, ZC),
            vmem(1, RANK),
            vmem(8, ZC),
            vmem(COLS, ZC),
            dma((NX // 4,)),
            dma((5,)),
            dma((2, 8)),
            dma((2, 8)),
            dma((5,)),
            dma((5,)),
        ],
        compiler_params=pltpu.CompilerParams(
            collective_id=0, has_side_effects=True, vmem_limit_bytes=40 * 2**20
        ),
        name="substeps",
    )(*given)
    out, factor, new = pl.pallas_call(
        finish_kernel,
        out_shape=(f32(19, NX, NY, NZ), f32(COLS, COLS), f32(COLS, ROWS, ZC)),
        in_specs=[here] * 6,
        out_specs=(far, here, far),
        scratch_shapes=[
            vmem(COLS, PITCH, ZC),
            vmem(COLS, ZC),
            vmem(ROWS, ZC),
            dma((ROWS // 16 + 2,)),
        ],
        compiler_params=pltpu.CompilerParams(vmem_limit_bytes=24 * 2**20),
        name="finish",
    )(field, stack, inverse, upper, border, left)
    return out, factor, new.reshape(COLS, 3, XC, YC, ZC)


def solution(mesh):
    return jax.shard_map(
        functools.partial(on_device, mesh.shape["gx"], mesh.shape["gy"]),
        mesh=mesh,
        in_specs=(
            P(None, "gx", "gy", None),
            P("gx", "gy", None),
            P("gx", "gy", None),
            P(),
            P(None, None, "gx", "gy", None),
            P(None, None, "gx", "gy", None),
        ),
        out_specs=(P(None, "gx", "gy", None), P(), P(None, None, "gx", "gy", None)),
        check_vma=False,
    )
```
